256 devices in a mesh: dp: 32 (over z, y), tensor: 8 (over x, core).
Axes of the slice: x: 4, y: 4, z: 8, core: 2. Of those that a mesh axis runs over, the one named last changes fastest.
Arguments:
- queries: bfloat16 [4, 3072, 64, 128], P(None, 'dp', 'tensor'), may hold values from -100 to 100
- stored_key_cache: bfloat16 [3072, 8, 48, 128], P('dp', 'tensor'), may hold values from -5 to 5
- stored_value_cache: bfloat16 [3072, 8, 48, 128], P('dp', 'tensor'), may hold values from -6 to 6
- fresh_token_keys: bfloat16 [4, 3072, 8, 128], P(None, 'dp', 'tensor'), may hold values from -6 to 6
- fresh_token_values: bfloat16 [4, 3072, 8, 128], P(None, 'dp', 'tensor'), may hold values from -6 to 6
- request_cache_length: int32 [3072], P('dp'), may hold values from 2 to 48, as said below
- output_projection_weight: bfloat16 [8192, 4096], P('tensor'), may hold values from -0.0625 to 0.0625
- adapter_shrink_weight: bfloat16 [128, 64, 8192], P('dp', None, 'tensor'), may hold values from -0.0625 to 0.0625
- adapter_expand_weight: bfloat16 [128, 64, 4096], P('dp', 'tensor'), may hold values from -0.75 to 0.75
- adapter_place_table: int32 [128], replicated, may hold values from 0 to 127, as said below
- adapter_fetch_table: int32 [1024], P('dp'), may hold values from 0 to 127, as said below
- request_fetch_entry: int32 [3072], P('dp'), may hold values from 0 to 31, as said below
Outputs:
- adapted: bfloat16 [4, 3072, 4096], P(None, 'dp', 'tensor')
The draws below stay inside these ranges and needn't reach their ends.
Inputs may be any that keep to these rules, and one draw needn't show every extreme that they name: `request_cache_length`: each cached length is 2 or more, and some request holds all 48 positions. `adapter_place_table`: A permutation of the adapter ids. `adapter_fetch_table`: the 32 ids of one index of dp are distinct, and at most 2 of them are stored (adapter_place_table // 4) by one index of dp; every index of dp reaches 2 for some owner. `request_fetch_entry`: every entry of an index's fetch list is used by some of its requests.
All inputs are finite; a program needn't handle non-finite values.
Results may differ from the reference program's by a relative error of at most 0.006.
Values may be sent and summed in bfloat16 or wider, within the bound.
A program may use at most 128 MiB of HBM per device.

```python
import jax
import jax.numpy as jnp
from jax import lax

QUERY_HEADS = 64
KVH = 8
HEAD_WIDTH = 128
OUTPUT_FEATURES = 4096
ADAPTER_RANK = 64
STEPS = 4
R_DEV = 96
CACHE = 48
ADP_DEV = 4
SLOTS = 32
ADAPTER_TOTAL = 128
REQUESTS = 3072
N_DP = 32


def owner_table(key):
    return jax.random.permutation(jax.random.fold_in(key, 11), ADAPTER_TOTAL).astype(jnp.int32)


def key_table(key):
    raw = jax.random.truncated_normal(jax.random.fold_in(key, 7), -4.0, 4.0, (REQUESTS, KVH, CACHE, HEAD_WIDTH), jnp.float32)
    second = raw[:, :, 1]
    return raw.at[:, :, 1].set(second)


def draw_adapter_place_table(key, part):
    return owner_table(key)


def draw_adapter_fetch_table(key, part):
    lookup_table = owner_table(key)
    key = jax.random.fold_in(key, 2)
    inverse = jnp.argsort(lookup_table).astype(jnp.int32)
    groups = ADAPTER_TOTAL // ADP_DEV

    def one_group(sub_key):
        key_order, key_pair, key_first, key_shift = jax.random.split(sub_key, 4)
        owner_order = jax.random.permutation(key_order, groups).astype(jnp.int32)
        slot_index = jnp.arange(SLOTS, dtype=jnp.int32)
        is_odd = slot_index % 2 == 1
        paired = jax.random.randint(key_pair, (SLOTS,), 0, 2, dtype=jnp.int32)
        paired = jnp.where(slot_index == 1, 1, paired)
        going_back = jnp.where(is_odd, paired, 0)
        owners = owner_order[slot_index - going_back]
        first_local = jax.random.randint(key_first, (SLOTS,), 0, ADP_DEV, dtype=jnp.int32)
        shifted = jax.random.randint(key_shift, (SLOTS,), 0, ADP_DEV - 1, dtype=jnp.int32)
        previous = jnp.roll(first_local, 1)
        within = jnp.where(going_back == 1, (previous + 1 + shifted) % ADP_DEV, first_local)
        return inverse[owners * ADP_DEV + within]
    return jax.vmap(one_group)(jax.random.split(key, groups)).reshape(-1).astype(jnp.int32)


def draw_request_fetch_entry(key, part):
    key = jax.random.fold_in(key, 3)
    groups = REQUESTS // R_DEV

    def one_group(sub_key):
        key_head, key_rest, key_order = jax.random.split(sub_key, 3)
        head_part = jax.random.permutation(key_head, SLOTS).astype(jnp.int32)
        rest_part = jax.random.randint(key_rest, (R_DEV - SLOTS,), 0, SLOTS, dtype=jnp.int32)
        return jax.random.permutation(key_order, jnp.concatenate([head_part, rest_part]))
    return jax.vmap(one_group)(jax.random.split(key, groups)).reshape(-1).astype(jnp.int32)


def draw_request_cache_length(key, part):
    key = jax.random.fold_in(key, 4)
    key_len, key_spot = jax.random.split(key)
    lengths = jax.random.randint(key_len, (REQUESTS,), 2, CACHE + 1, dtype=jnp.int32)
    spot = jax.random.randint(key_spot, (), 0, REQUESTS, dtype=jnp.int32)
    return jnp.where(jnp.arange(REQUESTS, dtype=jnp.int32) == spot, CACHE, lengths).astype(jnp.int32)


def draw_stored_key_cache(key, part):
    return key_table(key).astype(jnp.bfloat16)


def draw_queries(key, part):
    key = jax.random.fold_in(key, 8)
    values = jax.random.truncated_normal(key, -4.0, 4.0, (STEPS, REQUESTS, QUERY_HEADS, HEAD_WIDTH), jnp.float32)
    return values.astype(jnp.bfloat16)


def level_of(own_key, shape, cuts, smallest, top_value):
    gain, own = 1.0, jax.random.fold_in(own_key, 6)
    for dim, parts in cuts:
        draws = jnp.exp(jax.random.uniform(jax.random.fold_in(own, dim), (parts,), jnp.float32, smallest / len(cuts), top_value / len(cuts)))
        gain = gain * jnp.repeat(draws, shape[dim] // parts).reshape([-1 if axis == dim else 1 for axis in range(len(shape))])
    return gain


def noise(stream_key, shape, spread, limit, pieces=(), kind=jnp.bfloat16):
    values = spread * jax.random.normal(stream_key, shape, jnp.float32)
    if pieces:
        values = values * level_of(stream_key, shape, pieces, -0.22, 0.18)
    return jnp.clip(values, -limit, limit).astype(kind)


def setup_inputs(seed: int = 0) -> dict:
    seeds = jax.random.split(jax.random.key(seed), 13)
    queries = draw_queries(jax.random.fold_in(seeds[12], 71), 0)
    stored_key_cache = draw_stored_key_cache(jax.random.fold_in(seeds[12], 71), 0)
    stored_value_cache = noise(seeds[2], (REQUESTS, KVH, CACHE, HEAD_WIDTH), 1.0, 6.0, ((0, 32), (1, 8)))
    fresh_token_keys = noise(seeds[3], (STEPS, REQUESTS, KVH, HEAD_WIDTH), 1.0, 6.0, ((1, 32), (2, 8)))
    fresh_token_values = noise(seeds[4], (STEPS, REQUESTS, KVH, HEAD_WIDTH), 1.0, 6.0, ((1, 32), (2, 8)))
    request_cache_length = draw_request_cache_length(jax.random.fold_in(seeds[12], 71), 0)
    output_projection_weight = noise(seeds[6], (QUERY_HEADS * HEAD_WIDTH, OUTPUT_FEATURES), (QUERY_HEADS * HEAD_WIDTH) ** -0.5, 0.0625, ((0, 8),))
    adapter_shrink_weight = noise(seeds[7], (ADAPTER_TOTAL, ADAPTER_RANK, QUERY_HEADS * HEAD_WIDTH), (QUERY_HEADS * HEAD_WIDTH) ** -0.5, 0.0625, ((0, 32), (2, 8)))
    adapter_expand_weight = noise(seeds[8], (ADAPTER_TOTAL, ADAPTER_RANK, OUTPUT_FEATURES), ADAPTER_RANK ** -0.5, 0.75, ((0, 32), (1, 8)))
    adapter_place_table = draw_adapter_place_table(jax.random.fold_in(seeds[12], 71), 0)
    adapter_fetch_table = draw_adapter_fetch_table(jax.random.fold_in(seeds[12], 71), 0)
    request_fetch_entry = draw_request_fetch_entry(jax.random.fold_in(seeds[12], 71), 0)
    return {"queries": queries, "stored_key_cache": stored_key_cache, "stored_value_cache": stored_value_cache, "fresh_token_keys": fresh_token_keys, "fresh_token_values": fresh_token_values, "request_cache_length": request_cache_length, "output_projection_weight": output_projection_weight, "adapter_shrink_weight": adapter_shrink_weight, "adapter_expand_weight": adapter_expand_weight, "adapter_place_table": adapter_place_table, "adapter_fetch_table": adapter_fetch_table, "request_fetch_entry": request_fetch_entry}


def attend(queries, stored_key_cache, stored_value_cache, fresh_token_keys, fresh_token_values, request_cache_length):
    num_steps, num_rows, num_heads, head_size = queries.shape
    kv_heads = stored_key_cache.shape[1]
    cache_size = stored_key_cache.shape[2]
    grouped = queries.reshape(num_steps, num_rows, kv_heads, num_heads // kv_heads, head_size).astype(jnp.float32)
    score_scale = head_size ** -0.5
    on_cache = jnp.einsum("srkgd,rkcd->srkgc", grouped, stored_key_cache.astype(jnp.float32)) * score_scale
    on_new = jnp.einsum("srkgd,urkd->srkgu", grouped, fresh_token_keys.astype(jnp.float32)) * score_scale
    cache_live = (jnp.arange(cache_size, dtype=jnp.int32)[None, :] < request_cache_length[:, None])[None, :, None, None, :]
    new_live = (jnp.arange(num_steps)[None, :] <= jnp.arange(num_steps)[:, None])[:, None, None, None, :]
    on_cache = jnp.where(cache_live, on_cache, -jnp.inf)
    on_new = jnp.where(new_live, on_new, -jnp.inf)
    highest = jnp.maximum(jnp.max(on_cache, -1), jnp.max(on_new, -1))[..., None]
    exp_cache = jnp.exp(on_cache - highest)
    exp_new = jnp.exp(on_new - highest)
    weight_sum = jnp.sum(exp_cache, -1, keepdims=True) + jnp.sum(exp_new, -1, keepdims=True)
    weight_cache = (exp_cache / weight_sum).astype(jnp.bfloat16)
    weight_new = (exp_new / weight_sum).astype(jnp.bfloat16)
    attended_values = jnp.einsum("srkgc,rkcd->srkgd", weight_cache.astype(jnp.float32), stored_value_cache.astype(jnp.float32))
    attended_values = attended_values + jnp.einsum("srkgu,urkd->srkgd", weight_new.astype(jnp.float32), fresh_token_values.astype(jnp.float32))
    return attended_values.astype(jnp.bfloat16).reshape(num_steps, num_rows, num_heads * head_size)


def reference(queries, stored_key_cache, stored_value_cache, fresh_token_keys, fresh_token_values, request_cache_length, output_projection_weight, adapter_shrink_weight, adapter_expand_weight, adapter_place_table, adapter_fetch_table, request_fetch_entry):
    attended = attend(queries, stored_key_cache, stored_value_cache, fresh_token_keys, fresh_token_values, request_cache_length)
    features = attended.shape[2]
    base_part = jnp.dot(attended.reshape(STEPS * REQUESTS, features), output_projection_weight, preferred_element_type=jnp.float32)
    base_part = base_part.reshape(STEPS, REQUESTS, OUTPUT_FEATURES)
    grouped_rows = attended.reshape(STEPS, N_DP, R_DEV, features).transpose(1, 0, 2, 3)

    def per_group(inputs):
        ids_group, slots_group, rows_group = inputs
        adapter_ids = ids_group[slots_group]
        storage_places = adapter_place_table[adapter_ids]
        shrink_rows = adapter_shrink_weight[storage_places].astype(jnp.float32)
        expand_rows = adapter_expand_weight[storage_places].astype(jnp.float32)
        shrink = jnp.einsum("srd,rkd->srk", rows_group.astype(jnp.float32), shrink_rows).astype(jnp.bfloat16)
        return jnp.einsum("srk,rko->sro", shrink.astype(jnp.float32), expand_rows)

    expand = lax.map(per_group, (adapter_fetch_table.reshape(N_DP, SLOTS), request_fetch_entry.reshape(N_DP, R_DEV), grouped_rows))
    expand = expand.transpose(1, 0, 2, 3).reshape(STEPS, REQUESTS, OUTPUT_FEATURES)
    return (base_part + expand).astype(jnp.bfloat16)
```

```python
import functools

import jax
import jax.numpy as jnp
from jax import lax
from jax.experimental import pallas as pl
from jax.experimental.pallas import tpu as pltpu
from jax.sharding import PartitionSpec as P

MESH = pl.DeviceIdType.MESH
BF = jnp.bfloat16
F32 = jnp.float32
I32 = jnp.int32

NZ, NY, NX, NT = 8, 4, 4, 8
STEPS, REQ, HEADS, WIDTH, CACHE = 4, 96, 8, 128, 48
ROWS = STEPS * REQ
FEAT = HEADS * WIDTH
RANK, ADP = 64, 4
OUT = 512
PAIRS = REQ // 2
NQ = 2
W = OUT // NQ


def place():
    dp = lax.axis_index("dp")
    t = lax.axis_index("tensor")
    return dp // NY, dp % NY, t


def device(z, y, t):
    return {"dp": z * NY + y, "tensor": t}


def remote(src, dst, send, recv, to):
    return pltpu.make_async_remote_copy(
        src_ref=src, dst_ref=dst, send_sem=send, recv_sem=recv, device_id=to, device_id_type=MESH
    )


def kernel(
    q_hbm, k_hbm, v_hbm, fk_hbm, fv_hbm, len_ref, wo_hbm, a_hbm, b_hbm, table_ref, fetch_ref, entry_ref,
    o_ref,
    qv, kv, vv, fkv, fvv, fks, fvs, att, wo, lsem,
    ga, gb, sa, ra, sb, rb, st, rt,
    xg, plr, sx, rx, sp, rp,
    cs, cr, own, xs, xd, sc, rc, sxd, rxd,
    acc, vsh, sh_src, sh_rcv, sh_all, s1, r1, s2, r2,
    ex, ret_src, ret_rcv, fin, sr, rr,
):
    z, y, t = place()
    x, c = t // 2, t % 2
    up, down = device((z + 1) % NZ, y, t), device((z + NZ - 1) % NZ, y, t)
    yup, ydown = device(z, (y + 1) % NY, t), device(z, (y + NY - 1) % NY, t)

    def y_peer(o):
        return device(z, (y + o) % NY, t)

    def t_peer(o):
        return device(z, y, (t + o) % NT)

    def x_peer(o):
        return device(z, y, ((x + o) % NX) * 2 + c)

    sibling = device(z, y, x * 2 + 1 - c)

    loads = [
        pltpu.make_async_copy(q_hbm, qv, lsem.at[0]),
        pltpu.make_async_copy(k_hbm, kv, lsem.at[1]),
        pltpu.make_async_copy(v_hbm, vv, lsem.at[2]),
        pltpu.make_async_copy(fk_hbm, fkv, lsem.at[3]),
        pltpu.make_async_copy(fv_hbm, fvv, lsem.at[4]),
        pltpu.make_async_copy(a_hbm, ga.at[z], lsem.at[5]),
        pltpu.make_async_copy(wo_hbm, wo, lsem.at[6]),
    ]
    own_b = [
        pltpu.make_async_copy(
            b_hbm.at[:, pl.ds(pl.multiple_of(t * OUT + q * W, W), W)],
            gb.at[q, z, pl.ds(pl.multiple_of(t * 32, 32), 32)],
            lsem.at[7 + q],
        )
        for q in range(NQ)
    ]
    for copy in loads + own_b:
        copy.start()

    barrier = pltpu.get_barrier_semaphore()
    partners = [up, down] + [y_peer(o) for o in (1, 2, 3)] + [t_peer(o) for o in range(1, NT)]
    for to in partners:
        pl.semaphore_signal(barrier, inc=1, device_id=to, device_id_type=MESH)
    pl.semaphore_wait(barrier, len(partners))

    def ring_block(d, k):
        return (z - k + NZ) % NZ if d == 0 else (z + k) % NZ

    def a_copy(d, k, h):
        b = ring_block(d, k)
        part = pl.ds(h * 128, 128)
        src = a_hbm.at[part] if k == 0 else ga.at[b, part]
        return remote(src, ga.at[b, part], sa.at[d, k, h], ra.at[d, k, h], up if d == 0 else down)

    def a_used(d, k, h):
        return k < 3 or h == d

    def a_send(k, h):
        for d in (0, 1):
            if a_used(d, k, h):
                if k > 0:
                    a_copy(d, k - 1, h).wait_recv()
                a_copy(d, k, h).start()

    def b_copy(d, k, q):
        b = ring_block(d, k)
        ref = gb.at[q, b] if k < 3 else gb.at[q, b, pl.ds(d * 128, 128)]
        return remote(ref, ref, sb.at[d, k, q], rb.at[d, k, q], up if d == 0 else down)

    def b_send(k, q):
        for d in (0, 1):
            if k > 0:
                b_copy(d, k - 1, q).wait_recv()
            b_copy(d, k, q).start()

    def t_copy(o, q):
        return remote(
            b_hbm.at[:, pl.ds(pl.multiple_of(((t + o) % NT) * OUT + q * W, W), W)],
            gb.at[q, z, pl.ds(pl.multiple_of(t * 32, 32), 32)],
            st.at[o, q], rt.at[o, q], t_peer(o),
        )

    def t_arrived(o, q):
        b = gb.at[q, z, pl.ds(pl.multiple_of(((t - o + NT) % NT) * 32, 32), 32)]
        remote(b, b, st.at[o, q], rt.at[o, q], t_peer(o)).wait_recv()

    a_send(0, 0)
    a_send(0, 1)
    for q in range(NQ):
        for o in range(1, NT):
            t_copy(o, q).start()

    def place_row(r, carry):
        plr[y, pl.ds(r, 1), :] = jnp.full((1, 128), table_ref[fetch_ref[entry_ref[r]]], I32)
        return carry

    lax.fori_loop(0, REQ, place_row, 0, unroll=8)

    def p_copy(o):
        return remote(plr.at[y], plr.at[y], sp.at[o], rp.at[o], y_peer(o))

    def p_arrived(o):
        b = plr.at[(y - o + NY) % NY]
        remote(b, b, sp.at[o], rp.at[o], y_peer(o)).wait_recv()

    for o in (1, 2, 3):
        p_copy(o).start()

    for copy in loads[:5]:
        copy.wait()
    for u in range(STEPS):
        fks[pl.ds(u, REQ, stride=STEPS), :] = fkv[u].astype(F32)
        fvs[pl.ds(u, REQ, stride=STEPS), :] = fvv[u].astype(F32)

    row = lax.broadcasted_iota(I32, (64, 128), 0)
    col = lax.broadcasted_iota(I32, (64, 128), 1)
    row_step, row_req = row // 16, (row // 8) % 2
    cached, fresh = col < 96, (col >= 96) & (col < 104)
    same_cached = cached & ((col // CACHE) == row_req)
    same_fresh = fresh & (((col - 96) // STEPS) == row_req) & (((col - 96) % STEPS) <= row_step)
    position = jnp.where(same_cached, col % CACHE, jnp.where(same_fresh, 0, 1000))
    first = row_req == 0
    scale = WIDTH ** -0.5
    blank = jnp.zeros((24, 128), F32)

    def pair(p):
        eight = pl.ds(pl.multiple_of(p * 8, 8), 8)
        keys = jnp.concatenate(
            [kv[pl.ds(pl.multiple_of(p * 96, 32), 96), :], jnp.concatenate([fks[eight, :], blank], 0).astype(BF)], 0
        )
        values = jnp.concatenate(
            [vv[pl.ds(pl.multiple_of(p * 96, 32), 96), :], jnp.concatenate([fvs[eight, :], blank], 0).astype(BF)], 0
        )
        sixteen = pl.ds(pl.multiple_of(p * 16, 16), 16)
        queries = qv[:, sixteen, :].reshape(64, 128)
        scores = lax.dot_general(queries, keys, (((1,), (1,)), ((), ())), preferred_element_type=F32) * scale
        live = position < jnp.where(first, len_ref[2 * p], len_ref[2 * p + 1])
        scores = jnp.where(live, scores, -1e30)
        powers = jnp.exp(scores - jnp.max(scores, axis=1, keepdims=True))
        weights = (powers / jnp.sum(powers, axis=1, keepdims=True)).astype(BF)
        att[:, sixteen, :] = jnp.dot(weights, values, preferred_element_type=F32).reshape(STEPS, 16, 128)

    def pairs(lo, hi, n):
        def some(i, carry):
            for j in range(n):
                pair(lo + i * n + j)
            return carry

        lax.fori_loop(0, (hi - lo) // n, some, 0)

    pairs(0, PAIRS // 2, 4)
    a_send(1, 0)
    pairs(PAIRS // 2, PAIRS, 4)
    for s in range(STEPS):
        for h in range(HEADS):
            xg[y, s * REQ:(s + 1) * REQ, h * WIDTH:(h + 1) * WIDTH] = att[
                s, pl.ds(h, REQ, stride=HEADS), :
            ].astype(BF)

    def x_copy(d, k):
        to = yup if d == 0 else ydown
        if k == 0:
            ref = xg.at[y]
        else:
            ref = xg.at[(y + 3) % NY if d == 0 else (y + 1) % NY, pl.ds(d * (ROWS // 2), ROWS // 2)]
        return remote(ref, ref, sx.at[d, k], rx.at[d, k], to)

    x_copy(0, 0).start()
    x_copy(1, 0).start()
    a_send(1, 1)

    loads[6].wait()

    def weight(i, core):
        return wo[:, pl.ds(pl.multiple_of((i * 2 + core) * OUT, OUT), OUT)]

    def for_sibling(i, carry):
        cs[i] = jnp.dot(xg[y], weight(i, 1 - c), preferred_element_type=F32).astype(BF)
        return carry

    def for_own(i, carry):
        own[i] = jnp.dot(xg[y], weight(i, c), preferred_element_type=F32)
        return carry

    lax.fori_loop(0, NX, for_sibling, 0)
    c_copy = remote(cs, cr, sc.at[0], rc.at[0], sibling)
    c_copy.start()
    lax.fori_loop(0, NX, for_own, 0)
    a_send(2, 0)
    c_copy.wait_recv()

    def xd_copy(o):
        return remote(xs.at[o], xd.at[o], sxd.at[o], rxd.at[o], x_peer(o))

    for o in (2, 1, 3):
        xs[o] = (own[(x + o) % NX] + cr[(x + o) % NX].astype(F32)).astype(BF)
        xd_copy(o).start()
    a_send(2, 1)

    lane = lax.broadcasted_iota(I32, (REQ, 128), 1)

    def index_of(b):
        p = plr[b]
        return jnp.where(((p >> 2) & 3) == y, ((p >> 4) << 2) | (p & 3), -1000)

    def shrink(yb, zb):
        full = lax.dot_general(xg[yb], ga[zb], (((1,), (1,)), ((), ())), preferred_element_type=F32)
        v = vsh[yb]
        lower, upper = v == 4 * zb, v == 4 * zb + 2
        for s in range(STEPS):
            part = full[s * REQ:(s + 1) * REQ]
            acc[yb, s * REQ:(s + 1) * REQ, :] += jnp.where(lower, part[:, :128], 0.0) + jnp.where(
                upper, part[:, 128:], 0.0
            )

    def shrinks(yb, blocks):
        for zb in blocks:
            shrink(yb, zb)

    acc[...] = jnp.zeros_like(acc)
    vsh[y] = index_of(y) - jnp.where(lane >= 64, 1, 0)
    for o in (1, 2, 3):
        p_arrived(o)
        b = (y - o + NY) % NY
        vsh[b] = index_of(b) - jnp.where(lane >= 64, 1, 0)
    loads[5].wait()

    near = [z, (z + 7) % NZ, (z + 1) % NZ]
    shrinks(y, near)
    x_copy(0, 0).wait_recv()
    x_copy(0, 1).start()
    x_copy(1, 0).wait_recv()
    x_copy(1, 1).start()
    a_send(3, 0)
    for q in range(NQ):
        own_b[q].wait()
        for o in range(1, NT):
            t_arrived(o, q)
    b_send(0, 0)
    shrinks((y + 3) % NY, near)
    a_send(3, 1)
    b_send(0, 1)
    shrinks((y + 1) % NY, near)
    far = [(z + 6) % NZ, (z + 2) % NZ]
    for yb in (y, (y + 3) % NY, (y + 1) % NY):
        shrinks(yb, far)
    x_copy(0, 1).wait_recv()
    x_copy(1, 1).wait_recv()
    shrinks((y + 2) % NY, near + far)
    a_copy(0, 2, 1).wait_recv()
    a_copy(1, 2, 0).wait_recv()
    last = [(z + 5) % NZ, (z + 3) % NZ]
    for yb in range(NY):
        shrinks(yb, last)
    b_send(1, 0)
    a_copy(0, 3, 0).wait_recv()
    a_copy(1, 3, 1).wait_recv()
    for yb in range(NY):
        shrinks(yb, [(z + 4) % NZ])

    low = lax.broadcasted_iota(I32, (REQ, 128), 1) < 64
    for b in range(2):
        for s in range(STEPS):
            rows = pl.ds(s * REQ, REQ)
            a0, a1 = acc[b, rows, :], acc[b + 2, rows, :]
            a0 = a0 + pltpu.roll(a0, 64, 1)
            a1 = a1 + pltpu.roll(a1, 64, 1)
            sh_src[b * STEPS + s] = jnp.where(low, a0, a1)

    def s1_copy(o):
        return remote(sh_src.at[(t + o) % NT], sh_rcv.at[o], s1.at[o], r1.at[o], t_peer(o))

    for o in (4, 3, 5, 2, 6, 1, 7):
        s1_copy(o).start()
    b_send(1, 1)
    total = sh_src[t]
    for o in range(1, NT):
        s1_copy(o).wait_recv()
        total = total + sh_rcv[o]
    sh_all[t] = total.astype(BF)

    def s2_copy(o):
        return remote(sh_all.at[t], sh_all.at[t], s2.at[o], r2.at[o], t_peer(o))

    def s2_arrived(o):
        b = sh_all.at[(t - o + NT) % NT]
        remote(b, b, s2.at[o], r2.at[o], t_peer(o)).wait_recv()

    for o in (4, 3, 5, 2, 6, 1, 7):
        s2_copy(o).start()
    b_send(2, 0)
    fin[...] = own[x] + cr[x].astype(F32)
    for o in (1, 2, 3):
        xd_copy(o).wait_recv()
        fin[...] += xd[o].astype(F32)
    b_send(2, 1)
    for o in range(1, NT):
        s2_arrived(o)

    column = lax.broadcasted_iota(I32, (128, 256), 1)
    spread_row = lax.broadcasted_iota(I32, (128, 256), 0)
    adapter_of = (lax.broadcasted_iota(I32, (REQ, 256), 1) // 8) % ADP

    def spread(yb):
        half = yb // 2
        pick = jnp.where(
            spread_row == half * RANK + (column // 32) * 8 + column % 8, 1.0, 0.0
        ).astype(BF)
        index = index_of(yb)
        v = jnp.concatenate([index, index], axis=1) - adapter_of
        for s in range(STEPS):
            wide = jnp.dot(sh_all[(yb % 2) * STEPS + s], pick, preferred_element_type=F32)

            def one(zb, carry):
                cols = pl.ds(pl.multiple_of(zb * 256, 256), 256)
                ex[yb, s * REQ:(s + 1) * REQ, cols] = jnp.where(v == 4 * zb, wide, 0.0).astype(BF)
                return carry

            lax.fori_loop(0, NZ, one, 0)

    for o in (2, 1, 3, 0):
        spread((y + o) % NY)

    def ret_copy(o, q):
        return remote(ret_src.at[o, q], ret_rcv.at[o, q], sr.at[o, q], rr.at[o, q], y_peer(o))

    def b_last(k, q):
        for d in (0, 1):
            b_copy(d, k, q).wait_recv()

    b_send(3, 0)
    b_send(3, 1)
    for q in range(NQ):
        b_last(3, q)
        for o in (2, 1, 3):
            ret_src[o, q] = jnp.dot(
                ex[(y + o) % NY], gb[q].reshape(NZ * 256, W), preferred_element_type=F32
            ).astype(BF)
            ret_copy(o, q).start()
        fin[:, q * W:(q + 1) * W] += jnp.dot(
            ex[y], gb[q].reshape(NZ * 256, W), preferred_element_type=F32
        )
    for q in range(NQ):
        value = fin[:, q * W:(q + 1) * W]
        for o in (1, 2, 3):
            ret_copy(o, q).wait_recv()
            value = value + ret_rcv[o, q].astype(F32)
        o_ref[:, q * W:(q + 1) * W] = value.astype(BF)

    for d in (0, 1):
        for k in range(4):
            for h in range(2):
                if a_used(d, k, h):
                    a_copy(d, k, h).wait_send()
            for q in range(NQ):
                b_copy(d, k, q).wait_send()
        for k in range(2):
            x_copy(d, k).wait_send()
    for o in range(1, NT):
        for q in range(NQ):
            t_copy(o, q).wait_send()
        s1_copy(o).wait_send()
        s2_copy(o).wait_send()
    for o in (1, 2, 3):
        p_copy(o).wait_send()
        xd_copy(o).wait_send()
        for q in range(NQ):
            ret_copy(o, q).wait_send()
    c_copy.wait_send()


def on_device(q, k, v, fk, fv, lens, wo, a, b, table, fetch, entry):
    vmem, dma = pltpu.VMEM, pltpu.SemaphoreType.DMA
    hbm, smem = pl.BlockSpec(memory_space=pl.ANY), pl.BlockSpec(memory_space=pltpu.SMEM)
    scratch = [
        vmem((STEPS, REQ * HEADS, WIDTH), BF), vmem((REQ * CACHE, WIDTH), BF), vmem((REQ * CACHE, WIDTH), BF),
        vmem((STEPS, REQ, WIDTH), BF), vmem((STEPS, REQ, WIDTH), BF),
        vmem((ROWS, WIDTH), F32), vmem((ROWS, WIDTH), F32),
        vmem((STEPS, REQ * HEADS, WIDTH), F32), vmem((FEAT, NT * OUT), BF), dma((7 + NQ,)),
        vmem((NZ, 256, FEAT), BF), vmem((NQ, NZ, 256, W), BF),
        dma((2, 4, 2)), dma((2, 4, 2)), dma((2, 4, NQ)), dma((2, 4, NQ)), dma((NT, NQ)), dma((NT, NQ)),
        vmem((NY, ROWS, FEAT), BF), vmem((NY, REQ, 128), I32), dma((2, 2)), dma((2, 2)), dma((4,)), dma((4,)),
        vmem((NX, ROWS, OUT), BF), vmem((NX, ROWS, OUT), BF), vmem((NX, ROWS, OUT), F32),
        vmem((NX, ROWS, OUT), BF), vmem((NX, ROWS, OUT), BF), dma((1,)), dma((1,)), dma((4,)), dma((4,)),
        vmem((NY, ROWS, 128), F32), vmem((NY, REQ, 128), I32),
        vmem((NT, REQ, 128), F32), vmem((NT, REQ, 128), F32), vmem((NT, REQ, 128), BF),
        dma((NT,)), dma((NT,)), dma((NT,)), dma((NT,)),
        vmem((NY, ROWS, NZ * 256), BF), vmem((NY, NQ, ROWS, W), BF), vmem((NY, NQ, ROWS, W), BF),
        vmem((ROWS, OUT), F32), dma((4, NQ)), dma((4, NQ)),
    ]
    out = pl.pallas_call(
        kernel,
        out_shape=jax.ShapeDtypeStruct((ROWS, OUT), BF),
        in_specs=[hbm] * 5 + [smem] + [hbm] * 3 + [smem] * 3,
        out_specs=pl.BlockSpec(memory_space=vmem),
        scratch_shapes=scratch,
        compiler_params=pltpu.CompilerParams(
            collective_id=0, has_side_effects=True, vmem_limit_bytes=60 * 2**20
        ),
        name="lora_projection",
    )(
        q.reshape(STEPS, REQ * HEADS, WIDTH),
        k.reshape(REQ * CACHE, WIDTH),
        v.reshape(REQ * CACHE, WIDTH),
        fk.reshape(STEPS, REQ, WIDTH),
        fv.reshape(STEPS, REQ, WIDTH),
        lens,
        wo,
        a.reshape(ADP * RANK, FEAT),
        b.reshape(ADP * 8, NT * OUT),
        table,
        fetch,
        entry,
    )
    return out.reshape(STEPS, REQ, OUT)


def solution(mesh):
    return jax.shard_map(
        on_device,
        mesh=mesh,
        in_specs=(
            P(None, "dp", "tensor", None),
            P("dp", "tensor", None, None),
            P("dp", "tensor", None, None),
            P(None, "dp", "tensor", None),
            P(None, "dp", "tensor", None),
            P("dp"),
            P("tensor", None),
            P("dp", None, "tensor"),
            P("dp", "tensor", None),
            P(),
            P("dp"),
            P("dp"),
        ),
        out_specs=P(None, "dp", "tensor"),
        check_vma=False,
    )
```

```python
import functools

import jax
import jax.numpy as jnp
from jax import lax
from jax.experimental import pallas as pl
from jax.experimental.pallas import tpu as pltpu
from jax.sharding import PartitionSpec as P

MESH = pl.DeviceIdType.MESH
BF = jnp.bfloat16
F32 = jnp.float32
I32 = jnp.int32

NZ, NY, NX, NT = 8, 4, 4, 8
STEPS, REQ, HEADS, WIDTH, CACHE = 4, 96, 8, 128, 48
ROWS = STEPS * REQ
FEAT = HEADS * WIDTH
RANK, ADP = 64, 4
OUT, SLOTS = 512, 32
PAIRS = REQ // 2
CHUNKS = ((0, 256, 2), (256, 128, 1), (384, 128, 1))
NQ = len(CHUNKS)


def place():
    dp = lax.axis_index("dp")
    t = lax.axis_index("tensor")
    return dp // NY, dp % NY, t


def device(z, y, t):
    return {"dp": z * NY + y, "tensor": t}


def remote(src, dst, send, recv, to):
    return pltpu.make_async_remote_copy(
        src_ref=src, dst_ref=dst, send_sem=send, recv_sem=recv, device_id=to, device_id_type=MESH
    )


def kernel(
    q_hbm, k_hbm, v_hbm, fk_hbm, fv_hbm, len_hbm, wo_hbm, a_hbm, b_hbm, table_hbm, fetch_hbm, entry_hbm,
    o_hbm,
    len_ref, table_ref, fetch_ref, entry_ref, ssem, qv, kv, vv, fkv, fvv, fks, fvs, att, wo, lsem,
    ga, gb0, gb1, gb2, sa, ra, sb, rb, st, rt,
    xg, plr, sx, rx, sp, rp,
    cs, cr, own, xs, xd, sc, rc, sxd, rxd,
    acc, vsh, sh_src, sh_rcv, sh_all, s1, r1, s2, r2,
    ex, fs0, fs1, fs2, fr0, fr1, fr2, rs0, rs1, rs2, rr0, rr1, rr2, ov0, ov1, ov2, fin, sf, rf, sr, rr, osem,
):
    gb = (gb0, gb1, gb2)
    far_src, far_rcv = (fs0, fs1, fs2), (fr0, fr1, fr2)
    ret_src, ret_rcv, ov = (rs0, rs1, rs2), (rr0, rr1, rr2), (ov0, ov1, ov2)
    z, y, t = place()
    x, c = t // 2, t % 2
    up, down = device((z + 1) % NZ, y, t), device((z + NZ - 1) % NZ, y, t)
    yup, ydown = device(z, (y + 1) % NY, t), device(z, (y + NY - 1) % NY, t)

    def y_peer(o):
        return device(z, (y + o) % NY, t)

    def t_peer(o):
        return device(z, y, (t + o) % NT)

    def x_peer(o):
        return device(z, y, ((x + o) % NX) * 2 + c)

    sibling = device(z, y, x * 2 + 1 - c)

    loads = [
        pltpu.make_async_copy(q_hbm, qv, lsem.at[0]),
        pltpu.make_async_copy(k_hbm, kv, lsem.at[1]),
        pltpu.make_async_copy(v_hbm, vv, lsem.at[2]),
        pltpu.make_async_copy(fk_hbm, fkv, lsem.at[3]),
        pltpu.make_async_copy(fv_hbm, fvv, lsem.at[4]),
        pltpu.make_async_copy(a_hbm, ga.at[z], lsem.at[5]),
        pltpu.make_async_copy(wo_hbm, wo, lsem.at[6]),
    ]
    own_b = [
        pltpu.make_async_copy(
            b_hbm.at[:, pl.ds(pl.multiple_of(t * OUT + first, 128), width)],
            gb[q].at[z, pl.ds(pl.multiple_of(t * 32, 32), 32)],
            lsem.at[7 + q],
        )
        for q, (first, width, _) in enumerate(CHUNKS)
    ]
    tables = [
        pltpu.make_async_copy(entry_hbm, entry_ref, ssem.at[0]),
        pltpu.make_async_copy(fetch_hbm, fetch_ref, ssem.at[1]),
        pltpu.make_async_copy(table_hbm, table_ref, ssem.at[2]),
        pltpu.make_async_copy(len_hbm, len_ref, ssem.at[3]),
    ]

    barrier = pltpu.get_barrier_semaphore()
    partners = [up, down] + [y_peer(o) for o in (1, 2, 3)] + [t_peer(o) for o in range(1, NT)]
    for to in partners:
        pl.semaphore_signal(barrier, inc=1, device_id=to, device_id_type=MESH)
    for copy in tables + loads + own_b:
        copy.start()
    pl.semaphore_wait(barrier, len(partners))

    def ring_block(d, k):
        return (z - k + NZ) % NZ if d == 0 else (z + k) % NZ

    def a_copy(d, k, h):
        b = ring_block(d, k)
        part = pl.ds(h * 128, 128)
        src = a_hbm.at[part] if k == 0 else ga.at[b, part]
        return remote(src, ga.at[b, part], sa.at[d, k, h], ra.at[d, k, h], up if d == 0 else down)

    def a_used(d, k, h):
        return k < 3 or h == d

    def a_send(k, h):
        for d in (0, 1):
            if a_used(d, k, h):
                if k > 0:
                    a_copy(d, k - 1, h).wait_recv()
                a_copy(d, k, h).start()

    def b_copy(d, k, q, h=None):
        if CHUNKS[q][2] == 2:
            rows = pl.ds((d if k == 3 else h) * 128, 128)
        else:
            rows = pl.ds(d * 128, 128) if k == 3 else pl.ds(0, 256)
        ref, part = gb[q].at[ring_block(d, k), rows], h or 0
        return remote(ref, ref, sb.at[d, k, q, part], rb.at[d, k, q, part], up if d == 0 else down)

    def b_send(k, q, h=None):
        for d in (0, 1):
            if k > 0:
                b_copy(d, k - 1, q, d if k == 3 and CHUNKS[q][2] == 2 else h).wait_recv()
            b_copy(d, k, q, h).start()

    def b_arrived(q):
        for d in (0, 1):
            if CHUNKS[q][2] == 2:
                b_copy(d, 2, q, 1 - d).wait_recv()
            b_copy(d, 3, q).wait_recv()

    def b_sent(q):
        for d in (0, 1):
            for k in range(4):
                for h in (0, 1) if CHUNKS[q][2] == 2 and k < 3 else (None,):
                    b_copy(d, k, q, h).wait_send()

    def t_copy(o, q):
        first, width, _ = CHUNKS[q]
        return remote(
            b_hbm.at[:, pl.ds(pl.multiple_of(((t + o) % NT) * OUT + first, 128), width)],
            gb[q].at[z, pl.ds(pl.multiple_of(t * 32, 32), 32)],
            st.at[o, q], rt.at[o, q], t_peer(o),
        )

    def t_arrived(o, q):
        b = gb[q].at[z, pl.ds(pl.multiple_of(((t - o + NT) % NT) * 32, 32), 32)]
        remote(b, b, st.at[o, q], rt.at[o, q], t_peer(o)).wait_recv()

    a_send(0, 0)
    a_send(0, 1)
    for q in range(NQ):
        for o in range(1, NT):
            t_copy(o, q).start()

    def place_row(r, carry):
        plr[y, pl.ds(r, 1), :] = jnp.full((1, 128), table_ref[fetch_ref[entry_ref[r]]], I32)
        return carry

    for copy in tables:
        copy.wait()
    lax.fori_loop(0, REQ, place_row, 0, unroll=8)

    def p_copy(o):
        return remote(plr.at[y], plr.at[y], sp.at[o], rp.at[o], y_peer(o))

    def p_arrived(o):
        b = plr.at[(y - o + NY) % NY]
        remote(b, b, sp.at[o], rp.at[o], y_peer(o)).wait_recv()

    for o in (1, 2, 3):
        p_copy(o).start()

    for copy in loads[:5]:
        copy.wait()
    for u in range(STEPS):
        fks[pl.ds(u, REQ, stride=STEPS), :] = fkv[u].astype(F32)
        fvs[pl.ds(u, REQ, stride=STEPS), :] = fvv[u].astype(F32)

    row = lax.broadcasted_iota(I32, (64, 128), 0)
    col = lax.broadcasted_iota(I32, (64, 128), 1)
    row_step, row_req = row // 16, (row // 8) % 2
    cached, fresh = col < 96, (col >= 96) & (col < 104)
    same_cached = cached & ((col // CACHE) == row_req)
    same_fresh = fresh & (((col - 96) // STEPS) == row_req) & (((col - 96) % STEPS) <= row_step)
    position = jnp.where(same_cached, col % CACHE, jnp.where(same_fresh, 0, 1000))
    first = row_req == 0
    scale = WIDTH ** -0.5
    blank = jnp.zeros((24, 128), F32)

    def pair_group(ps):
        count = range(len(ps))
        eights = [pl.ds(pl.multiple_of(p * 8, 8), 8) for p in ps]
        rows = [pl.ds(pl.multiple_of(p * 96, 32), 96) for p in ps]
        sixteens = [pl.ds(pl.multiple_of(p * 16, 16), 16) for p in ps]

        def with_fresh(old, new, i):
            return jnp.concatenate(
                [old[rows[i], :], jnp.concatenate([new[eights[i], :], blank], 0).astype(BF)], 0
            )

        scores = [
            lax.dot_general(
                qv[:, sixteens[i], :].reshape(64, 128), with_fresh(kv, fks, i),
                (((1,), (1,)), ((), ())), preferred_element_type=F32,
            )
            for i in count
        ]
        live = [position < jnp.where(first, len_ref[2 * p], len_ref[2 * p + 1]) for p in ps]
        scores = [jnp.where(live[i], scores[i] * scale, -1e30) for i in count]
        highest = [jnp.max(v, axis=1, keepdims=True) for v in scores]
        powers = [jnp.exp(scores[i] - highest[i]) for i in count]
        sums = [jnp.sum(v, axis=1, keepdims=True) for v in powers]
        weights = [(powers[i] * (1.0 / sums[i])).astype(BF) for i in count]
        results = [
            jnp.dot(weights[i], with_fresh(vv, fvs, i), preferred_element_type=F32) for i in count
        ]
        for i in count:
            att[:, sixteens[i], :] = results[i].reshape(STEPS, 16, 128)

    def pairs(lo, hi, n):
        def some(i, carry):
            pair_group([lo + i * n + j for j in range(n)])
            return carry

        lax.fori_loop(0, (hi - lo) // n, some, 0)

    pairs(0, PAIRS // 2, 4)
    a_send(1, 0)
    pairs(PAIRS // 2, PAIRS, 4)
    for s in range(STEPS):
        for h in range(HEADS):
            xg[y, s * REQ:(s + 1) * REQ, h * WIDTH:(h + 1) * WIDTH] = att[
                s, pl.ds(h, REQ, stride=HEADS), :
            ].astype(BF)

    def x_copy(d, k):
        to = yup if d == 0 else ydown
        if k == 0:
            ref = xg.at[y]
        else:
            ref = xg.at[(y + 3) % NY if d == 0 else (y + 1) % NY, pl.ds(d * (ROWS // 2), ROWS // 2)]
        return remote(ref, ref, sx.at[d, k], rx.at[d, k], to)

    x_copy(0, 0).start()
    x_copy(1, 0).start()
    a_send(1, 1)

    loads[6].wait()

    def weight(i, core):
        return wo[:, pl.ds(pl.multiple_of((i * 2 + core) * OUT, OUT), OUT)]

    def for_sibling(i, carry):
        cs[i] = jnp.dot(xg[y], weight(i, 1 - c), preferred_element_type=F32).astype(BF)
        return carry

    def for_own(i, carry):
        own[i] = jnp.dot(xg[y], weight(i, c), preferred_element_type=F32)
        return carry

    lax.fori_loop(0, NX, for_sibling, 0)
    c_copy = remote(cs, cr, sc.at[0], rc.at[0], sibling)
    c_copy.start()
    lax.fori_loop(0, NX, for_own, 0)
    a_send(2, 0)
    c_copy.wait_recv()

    def xd_copy(o):
        return remote(xs.at[o], xd.at[o], sxd.at[o], rxd.at[o], x_peer(o))

    for o in (2, 1, 3):
        xs[o] = (own[(x + o) % NX] + cr[(x + o) % NX].astype(F32)).astype(BF)
        xd_copy(o).start()
    a_send(2, 1)

    lane = lax.broadcasted_iota(I32, (REQ, 128), 1)

    def index_of(b):
        p = plr[b]
        return jnp.where(((p >> 2) & 3) == y, ((p >> 4) << 2) | (p & 3), -1000)

    def shrink(yb, zb):
        full = lax.dot_general(xg[yb], ga[zb], (((1,), (1,)), ((), ())), preferred_element_type=F32)
        v = vsh[yb]
        lower, upper = v == 4 * zb, v == 4 * zb + 2
        for s in range(STEPS):
            part = full[s * REQ:(s + 1) * REQ]
            acc[yb, s * REQ:(s + 1) * REQ, :] += jnp.where(lower, part[:, :128], 0.0) + jnp.where(
                upper, part[:, 128:], 0.0
            )

    def shrinks(yb, blocks):
        for zb in blocks:
            shrink(yb, zb)

    acc[...] = jnp.zeros_like(acc)
    vsh[y] = index_of(y) - jnp.where(lane >= 64, 1, 0)
    for o in (1, 2, 3):
        p_arrived(o)
        b = (y - o + NY) % NY
        vsh[b] = index_of(b) - jnp.where(lane >= 64, 1, 0)
    loads[5].wait()

    near = [z, (z + 7) % NZ, (z + 1) % NZ]
    far = [(z + 6) % NZ, (z + 2) % NZ]
    last = [(z + 5) % NZ, (z + 3) % NZ]
    shrinks(y, near)
    x_copy(0, 0).wait_recv()
    x_copy(0, 1).start()
    x_copy(1, 0).wait_recv()
    x_copy(1, 1).start()
    a_send(3, 0)
    for q in range(NQ):
        own_b[q].wait()
        for o in range(1, NT):
            t_arrived(o, q)
    shrinks((y + 3) % NY, near)
    shrinks((y + 1) % NY, near)
    a_send(3, 1)
    b_send(0, 0, 0)
    b_send(0, 0, 1)
    b_send(0, 1)
    for yb in (y, (y + 3) % NY, (y + 1) % NY):
        shrinks(yb, far)
    x_copy(0, 1).wait_recv()
    x_copy(1, 1).wait_recv()
    shrinks((y + 2) % NY, near + far)
    a_copy(0, 2, 1).wait_recv()
    a_copy(1, 2, 0).wait_recv()
    for yb in range(NY):
        shrinks(yb, last)
    a_copy(0, 3, 0).wait_recv()
    a_copy(1, 3, 1).wait_recv()
    for yb in range(NY):
        shrinks(yb, [(z + 4) % NZ])

    low = lax.broadcasted_iota(I32, (REQ, 128), 1) < 64
    for b in range(2):
        for s in range(STEPS):
            rows = pl.ds(s * REQ, REQ)
            a0, a1 = acc[b, rows, :], acc[b + 2, rows, :]
            a0 = a0 + pltpu.roll(a0, 64, 1)
            a1 = a1 + pltpu.roll(a1, 64, 1)
            sh_src[b * STEPS + s] = jnp.where(low, a0, a1)

    def s1_copy(o):
        return remote(sh_src.at[(t + o) % NT], sh_rcv.at[o], s1.at[o], r1.at[o], t_peer(o))

    for o in (4, 3, 5, 2, 6, 1, 7):
        s1_copy(o).start()
    b_send(1, 0, 0)
    b_send(1, 0, 1)
    b_send(0, 2)
    fin[...] = own[x] + cr[x].astype(F32)
    for o in (1, 2, 3):
        xd_copy(o).wait_recv()
        fin[...] += xd[o].astype(F32)
    b_send(2, 0, 0)
    b_send(2, 0, 1)
    b_send(1, 1)
    total = sh_src[t]
    for o in range(1, NT):
        s1_copy(o).wait_recv()
        total = total + sh_rcv[o]
    sh_all[t] = total.astype(BF)

    def s2_copy(o):
        return remote(sh_all.at[t], sh_all.at[t], s2.at[o], r2.at[o], t_peer(o))

    def s2_arrived(o):
        b = sh_all.at[(t - o + NT) % NT]
        remote(b, b, s2.at[o], r2.at[o], t_peer(o)).wait_recv()

    for o in (4, 3, 5, 2, 6, 1, 7):
        s2_copy(o).start()
    b_send(3, 0)
    b_send(1, 2)
    for o in range(1, NT):
        s2_arrived(o)

    column = lax.broadcasted_iota(I32, (128, 256), 1)
    spread_row = lax.broadcasted_iota(I32, (128, 256), 0)
    adapter_of = (lax.broadcasted_iota(I32, (REQ, 256), 1) // 8) % ADP

    def spread(yb):
        half = yb // 2
        pick = jnp.where(
            spread_row == half * RANK + (column // 32) * 8 + column % 8, 1.0, 0.0
        ).astype(BF)
        index = index_of(yb)
        v = (jnp.concatenate([index, index], axis=1) - adapter_of).astype(F32).astype(BF)
        for s in range(STEPS):
            wide = jnp.dot(sh_all[(yb % 2) * STEPS + s], pick, preferred_element_type=F32).astype(BF)
            for zb in range(NZ):
                ex[yb, s * REQ:(s + 1) * REQ, zb * 256:(zb + 1) * 256] = jnp.where(
                    v == jnp.asarray(4 * zb, BF), wide, jnp.zeros_like(wide)
                )

    HALF = ROWS // 2
    top, bottom = pl.ds(0, HALF), pl.ds(HALF, HALF)

    def far_copy(d, q):
        return remote(far_src[q].at[d], far_rcv[q].at[d], sf.at[d, q], rf.at[d, q], yup if d == 0 else ydown)

    def ret_copy(d, h, q):
        rows = top if h == 0 else bottom
        return remote(
            ret_src[q].at[d, rows], ret_rcv[q].at[d, rows], sr.at[d, h, q], rr.at[d, h, q], yup if d == 0 else ydown
        )

    def columns(q):
        return slice(CHUNKS[q][0], CHUNKS[q][0] + CHUNKS[q][1])

    def expand(q, o):
        weights = gb[q][...].reshape(NZ * 256, CHUNKS[q][1])
        return jnp.dot(ex[(y + o) % NY], weights, preferred_element_type=F32)

    def give_far(q):
        value = expand(q, 2).astype(BF)
        for d in (0, 1):
            far_src[q][d] = value[d * HALF:(d + 1) * HALF]
            far_copy(d, q).start()

    def give_near(q):
        for d, o in ((0, 1), (1, 3)):
            ret_src[q][d] = expand(q, o).astype(BF)
            ret_copy(d, 1 - d, q).start()

    def pass_on(q):
        for d in (0, 1):
            far_copy(d, q).wait_recv()
            rows = top if d == 0 else bottom
            ret_src[q][d, rows, :] += far_rcv[q][d]
            ret_copy(d, d, q).start()

    def keep(q):
        fin[:, columns(q)] += expand(q, 0)

    spread((y + 2) % NY)
    b_send(2, 1)
    spread((y + 1) % NY)
    spread((y + 3) % NY)
    b_send(2, 2)
    b_arrived(0)
    give_far(0)
    b_send(3, 1)
    give_near(0)
    b_send(3, 2)
    spread(y)
    keep(0)
    pass_on(0)
    b_arrived(1)
    give_far(1)
    give_near(1)
    b_arrived(2)
    give_far(2)
    give_near(2)
    pass_on(1)
    pass_on(2)
    keep(1)
    keep(2)
    writes = []
    for q in range(NQ):
        value = fin[:, columns(q)]
        for d in (0, 1):
            for h in (0, 1):
                ret_copy(d, h, q).wait_recv()
            value = value + ret_rcv[q][d].astype(F32)
        ov[q][...] = value.astype(BF)
        writes.append(pltpu.make_async_copy(ov[q], o_hbm.at[:, columns(q)], osem.at[q]))
        writes[q].start()

    for d in (0, 1):
        for k in range(4):
            for h in range(2):
                if a_used(d, k, h):
                    a_copy(d, k, h).wait_send()
        for k in range(2):
            x_copy(d, k).wait_send()
        for q in range(NQ):
            far_copy(d, q).wait_send()
            for h in (0, 1):
                ret_copy(d, h, q).wait_send()
    for q in range(NQ):
        b_sent(q)
    for o in range(1, NT):
        for q in range(NQ):
            t_copy(o, q).wait_send()
        s1_copy(o).wait_send()
        s2_copy(o).wait_send()
    for o in (1, 2, 3):
        p_copy(o).wait_send()
        xd_copy(o).wait_send()
    c_copy.wait_send()
    for copy in writes:
        copy.wait()


def on_device(q, k, v, fk, fv, lens, wo, a, b, table, fetch, entry):
    vmem, dma = pltpu.VMEM, pltpu.SemaphoreType.DMA
    hbm, smem = pl.BlockSpec(memory_space=pl.ANY), pltpu.SMEM
    widths = [w for _, w, _ in CHUNKS]
    scratch = [
        smem((REQ,), I32), smem((NY * NZ * ADP,), I32), smem((SLOTS,), I32), smem((REQ,), I32), dma((4,)),
        vmem((STEPS, REQ * HEADS, WIDTH), BF), vmem((REQ * CACHE, WIDTH), BF), vmem((REQ * CACHE, WIDTH), BF),
        vmem((STEPS, REQ, WIDTH), BF), vmem((STEPS, REQ, WIDTH), BF),
        vmem((ROWS, WIDTH), F32), vmem((ROWS, WIDTH), F32),
        vmem((STEPS, REQ * HEADS, WIDTH), F32), vmem((FEAT, NT * OUT), BF), dma((7 + NQ,)),
        vmem((NZ, 256, FEAT), BF), *[vmem((NZ, 256, w), BF) for w in widths],
        dma((2, 4, 2)), dma((2, 4, 2)), dma((2, 4, NQ, 2)), dma((2, 4, NQ, 2)), dma((NT, NQ)), dma((NT, NQ)),
        vmem((NY, ROWS, FEAT), BF), vmem((NY, REQ, 128), I32), dma((2, 2)), dma((2, 2)), dma((4,)), dma((4,)),
        vmem((NX, ROWS, OUT), BF), vmem((NX, ROWS, OUT), BF), vmem((NX, ROWS, OUT), F32),
        vmem((NX, ROWS, OUT), BF), vmem((NX, ROWS, OUT), BF), dma((1,)), dma((1,)), dma((4,)), dma((4,)),
        vmem((NY, ROWS, 128), F32), vmem((NY, REQ, 128), I32),
        vmem((NT, REQ, 128), F32), vmem((NT, REQ, 128), F32), vmem((NT, REQ, 128), BF),
        dma((NT,)), dma((NT,)), dma((NT,)), dma((NT,)),
        vmem((NY, ROWS, NZ * 256), BF),
        *[vmem((2, ROWS // 2, w), BF) for w in widths * 2],
        *[vmem((2, ROWS, w), BF) for w in widths * 2],
        *[vmem((ROWS, w), BF) for w in widths],
        vmem((ROWS, OUT), F32), dma((2, NQ)), dma((2, NQ)), dma((2, 2, NQ)), dma((2, 2, NQ)), dma((NQ,)),
    ]
    out = pl.pallas_call(
        kernel,
        out_shape=jax.ShapeDtypeStruct((ROWS, OUT), BF),
        in_specs=[hbm] * 12,
        out_specs=hbm,
        scratch_shapes=scratch,
        compiler_params=pltpu.CompilerParams(
            collective_id=0, has_side_effects=True, vmem_limit_bytes=60 * 2**20
        ),
        name="lora_projection",
    )(
        q.reshape(STEPS, REQ * HEADS, WIDTH),
        k.reshape(REQ * CACHE, WIDTH),
        v.reshape(REQ * CACHE, WIDTH),
        fk.reshape(STEPS, REQ, WIDTH),
        fv.reshape(STEPS, REQ, WIDTH),
        lens,
        wo,
        a.reshape(ADP * RANK, FEAT),
        b.reshape(ADP * 8, NT * OUT),
        table,
        fetch,
        entry,
    )
    return out.reshape(STEPS, REQ, OUT)


def solution(mesh):
    return jax.shard_map(
        on_device,
        mesh=mesh,
        in_specs=(
            P(None, "dp", "tensor", None),
            P("dp", "tensor", None, None),
            P("dp", "tensor", None, None),
            P(None, "dp", "tensor", None),
            P(None, "dp", "tensor", None),
            P("dp"),
            P("tensor", None),
            P("dp", None, "tensor"),
            P("dp", "tensor", None),
            P(),
            P("dp"),
            P("dp"),
        ),
        out_specs=P(None, "dp", "tensor"),
        check_vma=False,
    )
```

```python
import functools

import jax
import jax.numpy as jnp
from jax import lax
from jax.experimental import pallas as pl
from jax.experimental.pallas import tpu as pltpu
from jax.sharding import PartitionSpec as P

MESH = pl.DeviceIdType.MESH
BF = jnp.bfloat16
F32 = jnp.float32
I32 = jnp.int32

NZ, NY, NX, NT = 8, 4, 4, 8
STEPS, REQ, HEADS, WIDTH, CACHE = 4, 96, 8, 128, 48
ROWS = STEPS * REQ
FEAT = HEADS * WIDTH
RANK, ADP = 64, 4
OUT, SLOTS = 512, 32
PAIRS = REQ // 2
CHUNKS = ((0, 256, 2), (256, 256, 2))
NQ = len(CHUNKS)


def place():
    dp = lax.axis_index("dp")
    t = lax.axis_index("tensor")
    return dp // NY, dp % NY, t


def device(z, y, t):
    return {"dp": z * NY + y, "tensor": t}


def remote(src, dst, send, recv, to):
    return pltpu.make_async_remote_copy(
        src_ref=src, dst_ref=dst, send_sem=send, recv_sem=recv, device_id=to, device_id_type=MESH
    )


def kernel(
    q_hbm, k_hbm, v_hbm, fk_hbm, fv_hbm, len_hbm, wo_hbm, a_hbm, b_hbm, table_hbm, fetch_hbm, entry_hbm,
    o_hbm,
    len_ref, table_ref, fetch_ref, entry_ref, ssem, qv, kv, vv, fkv, fvv, fks, fvs, att, wo, lsem,
    ga, gb0, gb1, sa, ra, sb, rb, st, rt,
    xg, plr, sx, rx, sp, rp,
    cs, cr, own, xs, xd, sc, rc, sxd, rxd,
    acc, vsh, sh_src, sh_rcv, sh_all, s1, r1, s2, r2,
    ex, fs0, fs1, fr0, fr1, rs0, rs1, rr0, rr1, ov0, ov1, fin, sf, rf, sr, rr, osem,
):
    gb = (gb0, gb1)
    far_src, far_rcv = (fs0, fs1), (fr0, fr1)
    ret_src, ret_rcv, ov = (rs0, rs1), (rr0, rr1), (ov0, ov1)
    z, y, t = place()
    x, c = t // 2, t % 2
    up, down = device((z + 1) % NZ, y, t), device((z + NZ - 1) % NZ, y, t)
    yup, ydown = device(z, (y + 1) % NY, t), device(z, (y + NY - 1) % NY, t)

    def y_peer(o):
        return device(z, (y + o) % NY, t)

    def t_peer(o):
        return device(z, y, (t + o) % NT)

    def x_peer(o):
        return device(z, y, ((x + o) % NX) * 2 + c)

    sibling = device(z, y, x * 2 + 1 - c)

    loads = [
        pltpu.make_async_copy(q_hbm, qv, lsem.at[0]),
        pltpu.make_async_copy(k_hbm, kv, lsem.at[1]),
        pltpu.make_async_copy(v_hbm, vv, lsem.at[2]),
        pltpu.make_async_copy(fk_hbm, fkv, lsem.at[3]),
        pltpu.make_async_copy(fv_hbm, fvv, lsem.at[4]),
        pltpu.make_async_copy(a_hbm, ga.at[z], lsem.at[5]),
        pltpu.make_async_copy(wo_hbm, wo, lsem.at[6]),
    ]
    own_b = [
        pltpu.make_async_copy(
            b_hbm.at[:, pl.ds(pl.multiple_of(t * OUT + first, 128), width)],
            gb[q].at[z, pl.ds(pl.multiple_of(t * 32, 32), 32)],
            lsem.at[7 + q],
        )
        for q, (first, width, _) in enumerate(CHUNKS)
    ]
    tables = [
        pltpu.make_async_copy(entry_hbm, entry_ref, ssem.at[0]),
        pltpu.make_async_copy(fetch_hbm, fetch_ref, ssem.at[1]),
        pltpu.make_async_copy(table_hbm, table_ref, ssem.at[2]),
        pltpu.make_async_copy(len_hbm, len_ref, ssem.at[3]),
    ]

    barrier = pltpu.get_barrier_semaphore()
    partners = [up, down] + [y_peer(o) for o in (1, 2, 3)] + [t_peer(o) for o in range(1, NT)]
    for to in partners:
        pl.semaphore_signal(barrier, inc=1, device_id=to, device_id_type=MESH)
    for copy in tables + loads + own_b:
        copy.start()
    pl.semaphore_wait(barrier, len(partners))

    def ring_block(d, k):
        return (z - k + NZ) % NZ if d == 0 else (z + k) % NZ

    def a_copy(d, k, h):
        b = ring_block(d, k)
        part = pl.ds(h * 128, 128)
        src = a_hbm.at[part] if k == 0 else ga.at[b, part]
        return remote(src, ga.at[b, part], sa.at[d, k, h], ra.at[d, k, h], up if d == 0 else down)

    def a_used(d, k, h):
        return k < 3 or h == d

    def a_send(k, i):
        for d, h in ((0, i), (1, 1 - i)):
            if a_used(d, k, h):
                if k > 0:
                    a_copy(d, k - 1, h).wait_recv()
                a_copy(d, k, h).start()

    def b_copy(d, k, q, h=None):
        if CHUNKS[q][2] == 2:
            rows = pl.ds((d if k == 3 else h) * 128, 128)
        else:
            rows = pl.ds(d * 128, 128) if k == 3 else pl.ds(0, 256)
        ref, part = gb[q].at[ring_block(d, k), rows], h or 0
        return remote(ref, ref, sb.at[d, k, q, part], rb.at[d, k, q, part], up if d == 0 else down)

    def b_send(k, q, i=None):
        for d in (0, 1):
            h = i if i is None or d == 0 else 1 - i
            if k > 0:
                b_copy(d, k - 1, q, d if k == 3 and CHUNKS[q][2] == 2 else h).wait_recv()
            b_copy(d, k, q, h).start()

    def b_arrived(q):
        for d in (0, 1):
            if CHUNKS[q][2] == 2:
                b_copy(d, 2, q, 1 - d).wait_recv()
            b_copy(d, 3, q).wait_recv()

    def b_sent(q):
        for d in (0, 1):
            for k in range(4):
                for h in (0, 1) if CHUNKS[q][2] == 2 and k < 3 else (None,):
                    b_copy(d, k, q, h).wait_send()

    def t_copy(o, q):
        first, width, _ = CHUNKS[q]
        return remote(
            b_hbm.at[:, pl.ds(pl.multiple_of(((t + o) % NT) * OUT + first, 128), width)],
            gb[q].at[z, pl.ds(pl.multiple_of(t * 32, 32), 32)],
            st.at[o, q], rt.at[o, q], t_peer(o),
        )

    def t_arrived(o, q):
        b = gb[q].at[z, pl.ds(pl.multiple_of(((t - o + NT) % NT) * 32, 32), 32)]
        remote(b, b, st.at[o, q], rt.at[o, q], t_peer(o)).wait_recv()

    a_send(0, 0)
    a_send(0, 1)
    for q in range(NQ):
        for o in range(1, NT):
            t_copy(o, q).start()

    def place_row(r, carry):
        plr[y, pl.ds(r, 1), :] = jnp.full((1, 128), table_ref[fetch_ref[entry_ref[r]]], I32)
        return carry

    for copy in tables:
        copy.wait()
    lax.fori_loop(0, REQ, place_row, 0, unroll=8)

    def p_copy(o):
        return remote(plr.at[y], plr.at[y], sp.at[o], rp.at[o], y_peer(o))

    def p_arrived(o):
        b = plr.at[(y - o + NY) % NY]
        remote(b, b, sp.at[o], rp.at[o], y_peer(o)).wait_recv()

    for o in (1, 2, 3):
        p_copy(o).start()

    for copy in loads[:5]:
        copy.wait()
    for u in range(STEPS):
        fks[pl.ds(u, REQ, stride=STEPS), :] = fkv[u].astype(F32)
        fvs[pl.ds(u, REQ, stride=STEPS), :] = fvv[u].astype(F32)

    row = lax.broadcasted_iota(I32, (64, 128), 0)
    col = lax.broadcasted_iota(I32, (64, 128), 1)
    row_step, row_req = row // 16, (row // 8) % 2
    cached, fresh = col < 96, (col >= 96) & (col < 104)
    same_cached = cached & ((col // CACHE) == row_req)
    same_fresh = fresh & (((col - 96) // STEPS) == row_req) & (((col - 96) % STEPS) <= row_step)
    position = jnp.where(same_cached, col % CACHE, jnp.where(same_fresh, 0, 1000))
    first = row_req == 0
    scale = WIDTH ** -0.5
    blank = jnp.zeros((24, 128), F32)

    def pair_group(ps):
        count = range(len(ps))
        eights = [pl.ds(pl.multiple_of(p * 8, 8), 8) for p in ps]
        rows = [pl.ds(pl.multiple_of(p * 96, 32), 96) for p in ps]
        sixteens = [pl.ds(pl.multiple_of(p * 16, 16), 16) for p in ps]

        def with_fresh(old, new, i):
            return jnp.concatenate(
                [old[rows[i], :], jnp.concatenate([new[eights[i], :], blank], 0).astype(BF)], 0
            )

        scores = [
            lax.dot_general(
                qv[:, sixteens[i], :].reshape(64, 128), with_fresh(kv, fks, i),
                (((1,), (1,)), ((), ())), preferred_element_type=F32,
            )
            for i in count
        ]
        live = [position < jnp.where(first, len_ref[2 * p], len_ref[2 * p + 1]) for p in ps]
        scores = [jnp.where(live[i], scores[i] * scale, -1e30) for i in count]
        highest = [jnp.max(v, axis=1, keepdims=True) for v in scores]
        powers = [jnp.exp(scores[i] - highest[i]) for i in count]
        sums = [jnp.sum(v, axis=1, keepdims=True) for v in powers]
        weights = [(powers[i] * (1.0 / sums[i])).astype(BF) for i in count]
        results = [
            jnp.dot(weights[i], with_fresh(vv, fvs, i), preferred_element_type=F32) for i in count
        ]
        for i in count:
            att[:, sixteens[i], :] = results[i].reshape(STEPS, 16, 128)

    def pairs(lo, hi, n):
        def some(i, carry):
            pair_group([lo + i * n + j for j in range(n)])
            return carry

        lax.fori_loop(0, (hi - lo) // n, some, 0)

    pairs(0, PAIRS // 2, 4)
    a_send(1, 0)
    pairs(PAIRS // 2, PAIRS, 4)
    for s in range(STEPS):
        for h in range(HEADS):
            xg[y, s * REQ:(s + 1) * REQ, h * WIDTH:(h + 1) * WIDTH] = att[
                s, pl.ds(h, REQ, stride=HEADS), :
            ].astype(BF)

    def x_copy(d, k):
        to = yup if d == 0 else ydown
        if k == 0:
            ref = xg.at[y]
        else:
            ref = xg.at[(y + 3) % NY if d == 0 else (y + 1) % NY, pl.ds(d * (ROWS // 2), ROWS // 2)]
        return remote(ref, ref, sx.at[d, k], rx.at[d, k], to)

    x_copy(0, 0).start()
    x_copy(1, 0).start()
    a_send(1, 1)

    loads[6].wait()

    def weight(i, core):
        return wo[:, pl.ds(pl.multiple_of((i * 2 + core) * OUT, OUT), OUT)]

    def for_sibling(i, carry):
        cs[i] = jnp.dot(xg[y], weight(i, 1 - c), preferred_element_type=F32).astype(BF)
        return carry

    def for_own(i, carry):
        own[i] = jnp.dot(xg[y], weight(i, c), preferred_element_type=F32)
        return carry

    lax.fori_loop(0, NX, for_sibling, 0)
    c_copy = remote(cs, cr, sc.at[0], rc.at[0], sibling)
    c_copy.start()
    lax.fori_loop(0, NX, for_own, 0)
    a_send(2, 0)
    c_copy.wait_recv()

    def xd_copy(o):
        return remote(xs.at[o], xd.at[o], sxd.at[o], rxd.at[o], x_peer(o))

    for o in (2, 1, 3):
        xs[o] = (own[(x + o) % NX] + cr[(x + o) % NX].astype(F32)).astype(BF)
        xd_copy(o).start()
    a_send(2, 1)

    lane = lax.broadcasted_iota(I32, (REQ, 128), 1)

    def index_of(b):
        p = plr[b]
        return jnp.where(((p >> 2) & 3) == y, ((p >> 4) << 2) | (p & 3), -1000)

    def shrink(yb, zb):
        full = lax.dot_general(xg[yb], ga[zb], (((1,), (1,)), ((), ())), preferred_element_type=F32)
        v = vsh[yb]
        lower, upper = v == 4 * zb, v == 4 * zb + 2
        for s in range(STEPS):
            part = full[s * REQ:(s + 1) * REQ]
            acc[yb, s * REQ:(s + 1) * REQ, :] += jnp.where(lower, part[:, :128], 0.0) + jnp.where(
                upper, part[:, 128:], 0.0
            )

    def shrinks(yb, blocks):
        for zb in blocks:
            shrink(yb, zb)

    acc[...] = jnp.zeros_like(acc)
    vsh[y] = index_of(y) - jnp.where(lane >= 64, 1, 0)
    for o in (1, 2, 3):
        p_arrived(o)
        b = (y - o + NY) % NY
        vsh[b] = index_of(b) - jnp.where(lane >= 64, 1, 0)
    loads[5].wait()

    near = [z, (z + 7) % NZ, (z + 1) % NZ]
    far = [(z + 6) % NZ, (z + 2) % NZ]
    last = [(z + 5) % NZ, (z + 3) % NZ]
    shrinks(y, near)
    for q in range(NQ):
        own_b[q].wait()
        for o in range(1, NT):
            t_arrived(o, q)
    b_send(0, 0, 0)
    x_copy(0, 0).wait_recv()
    x_copy(0, 1).start()
    x_copy(1, 0).wait_recv()
    x_copy(1, 1).start()
    a_send(3, 0)
    b_send(0, 0, 1)
    b_send(0, 1, 0)
    shrinks((y + 3) % NY, near)
    shrinks((y + 1) % NY, near)
    for yb in (y, (y + 3) % NY, (y + 1) % NY):
        shrinks(yb, far)
    x_copy(0, 1).wait_recv()
    x_copy(1, 1).wait_recv()
    shrinks((y + 2) % NY, near + far)
    b_send(1, 0, 0)
    b_send(1, 0, 1)
    a_copy(0, 2, 1).wait_recv()
    a_copy(1, 2, 0).wait_recv()
    for yb in range(NY):
        shrinks(yb, last)
    b_send(1, 1, 0)
    a_copy(0, 3, 0).wait_recv()
    a_copy(1, 3, 1).wait_recv()
    for yb in range(NY):
        shrinks(yb, [(z + 4) % NZ])

    low = lax.broadcasted_iota(I32, (REQ, 128), 1) < 64
    for b in range(2):
        for s in range(STEPS):
            rows = pl.ds(s * REQ, REQ)
            a0, a1 = acc[b, rows, :], acc[b + 2, rows, :]
            a0 = a0 + pltpu.roll(a0, 64, 1)
            a1 = a1 + pltpu.roll(a1, 64, 1)
            sh_src[b * STEPS + s] = jnp.where(low, a0, a1).astype(BF)

    def s1_copy(o):
        return remote(sh_src.at[(t + o) % NT], sh_rcv.at[o], s1.at[o], r1.at[o], t_peer(o))

    for o in (4, 3, 5, 2, 6, 1, 7):
        s1_copy(o).start()
    b_send(2, 0, 0)
    b_send(2, 0, 1)
    b_send(0, 1, 1)
    fin[...] = own[x] + cr[x].astype(F32)
    for o in (1, 2, 3):
        xd_copy(o).wait_recv()
        fin[...] += xd[o].astype(F32)
    total = sh_src[t].astype(F32)
    for o in range(1, NT):
        s1_copy(o).wait_recv()
        total = total + sh_rcv[o].astype(F32)
    sh_all[t] = total.astype(BF)

    def s2_copy(o):
        return remote(sh_all.at[t], sh_all.at[t], s2.at[o], r2.at[o], t_peer(o))

    def s2_arrived(o):
        b = sh_all.at[(t - o + NT) % NT]
        remote(b, b, s2.at[o], r2.at[o], t_peer(o)).wait_recv()

    for o in (4, 3, 5, 2, 6, 1, 7):
        s2_copy(o).start()
    b_send(3, 0)
    b_send(2, 1, 0)
    b_send(1, 1, 1)
    for o in range(1, NT):
        s2_arrived(o)

    column = lax.broadcasted_iota(I32, (128, 256), 1)
    spread_row = lax.broadcasted_iota(I32, (128, 256), 0)
    adapter_of = (lax.broadcasted_iota(I32, (REQ, 256), 1) // 8) % ADP

    def spread(yb):
        half = yb // 2
        pick = jnp.where(
            spread_row == half * RANK + (column // 32) * 8 + column % 8, 1.0, 0.0
        ).astype(BF)
        index = index_of(yb)
        v = (jnp.concatenate([index, index], axis=1) - adapter_of).astype(F32).astype(BF)
        for s in range(STEPS):
            wide = jnp.dot(sh_all[(yb % 2) * STEPS + s], pick, preferred_element_type=F32).astype(BF)
            for zb in range(NZ):
                ex[yb, s * REQ:(s + 1) * REQ, zb * 256:(zb + 1) * 256] = jnp.where(
                    v == jnp.asarray(4 * zb, BF), wide, jnp.zeros_like(wide)
                )

    HALF = ROWS // 2
    top, bottom = pl.ds(0, HALF), pl.ds(HALF, HALF)

    def far_copy(d, q):
        return remote(far_src[q].at[d], far_rcv[q].at[d], sf.at[d, q], rf.at[d, q], yup if d == 0 else ydown)

    def ret_copy(d, h, q):
        rows = top if h == 0 else bottom
        return remote(
            ret_src[q].at[d, rows], ret_rcv[q].at[d, rows], sr.at[d, h, q], rr.at[d, h, q], yup if d == 0 else ydown
        )

    def columns(q):
        return slice(CHUNKS[q][0], CHUNKS[q][0] + CHUNKS[q][1])

    def expand(q, o):
        weights = gb[q][...].reshape(NZ * 256, CHUNKS[q][1])
        return jnp.dot(ex[(y + o) % NY], weights, preferred_element_type=F32)

    def give_far(q):
        value = expand(q, 2).astype(BF)
        for d in (0, 1):
            far_src[q][d] = value[d * HALF:(d + 1) * HALF]
            far_copy(d, q).start()

    def give_near(q):
        for d, o in ((0, 1), (1, 3)):
            ret_src[q][d] = expand(q, o).astype(BF)
            ret_copy(d, 1 - d, q).start()

    def pass_on(q):
        for d in (0, 1):
            far_copy(d, q).wait_recv()
            rows = top if d == 0 else bottom
            ret_src[q][d, rows, :] += far_rcv[q][d]
            ret_copy(d, d, q).start()

    def keep(q):
        fin[:, columns(q)] += expand(q, 0)

    spread((y + 2) % NY)
    b_arrived(0)
    give_far(0)
    spread((y + 1) % NY)
    spread((y + 3) % NY)
    b_send(3, 1)
    give_near(0)
    b_send(2, 1, 1)
    spread(y)
    keep(0)
    pass_on(0)
    b_arrived(1)
    give_far(1)
    give_near(1)
    keep(1)
    pass_on(1)
    writes = []
    for q in range(NQ):
        value = fin[:, columns(q)]
        for d in (0, 1):
            for h in (0, 1):
                ret_copy(d, h, q).wait_recv()
            value = value + ret_rcv[q][d].astype(F32)
        ov[q][...] = value.astype(BF)
        writes.append(pltpu.make_async_copy(ov[q], o_hbm.at[:, columns(q)], osem.at[q]))
        writes[q].start()

    for d in (0, 1):
        for k in range(4):
            for h in range(2):
                if a_used(d, k, h):
                    a_copy(d, k, h).wait_send()
        for k in range(2):
            x_copy(d, k).wait_send()
        for q in range(NQ):
            far_copy(d, q).wait_send()
            for h in (0, 1):
                ret_copy(d, h, q).wait_send()
    for q in range(NQ):
        b_sent(q)
    for o in range(1, NT):
        for q in range(NQ):
            t_copy(o, q).wait_send()
        s1_copy(o).wait_send()
        s2_copy(o).wait_send()
    for o in (1, 2, 3):
        p_copy(o).wait_send()
        xd_copy(o).wait_send()
    c_copy.wait_send()
    for copy in writes:
        copy.wait()


def on_device(q, k, v, fk, fv, lens, wo, a, b, table, fetch, entry):
    vmem, dma = pltpu.VMEM, pltpu.SemaphoreType.DMA
    hbm, smem = pl.BlockSpec(memory_space=pl.ANY), pltpu.SMEM
    widths = [w for _, w, _ in CHUNKS]
    scratch = [
        smem((REQ,), I32), smem((NY * NZ * ADP,), I32), smem((SLOTS,), I32), smem((REQ,), I32), dma((4,)),
        vmem((STEPS, REQ * HEADS, WIDTH), BF), vmem((REQ * CACHE, WIDTH), BF), vmem((REQ * CACHE, WIDTH), BF),
        vmem((STEPS, REQ, WIDTH), BF), vmem((STEPS, REQ, WIDTH), BF),
        vmem((ROWS, WIDTH), F32), vmem((ROWS, WIDTH), F32),
        vmem((STEPS, REQ * HEADS, WIDTH), F32), vmem((FEAT, NT * OUT), BF), dma((7 + NQ,)),
        vmem((NZ, 256, FEAT), BF), *[vmem((NZ, 256, w), BF) for w in widths],
        dma((2, 4, 2)), dma((2, 4, 2)), dma((2, 4, NQ, 2)), dma((2, 4, NQ, 2)), dma((NT, NQ)), dma((NT, NQ)),
        vmem((NY, ROWS, FEAT), BF), vmem((NY, REQ, 128), I32), dma((2, 2)), dma((2, 2)), dma((4,)), dma((4,)),
        vmem((NX, ROWS, OUT), BF), vmem((NX, ROWS, OUT), BF), vmem((NX, ROWS, OUT), F32),
        vmem((NX, ROWS, OUT), BF), vmem((NX, ROWS, OUT), BF), dma((1,)), dma((1,)), dma((4,)), dma((4,)),
        vmem((NY, ROWS, 128), F32), vmem((NY, REQ, 128), I32),
        vmem((NT, REQ, 128), BF), vmem((NT, REQ, 128), BF), vmem((NT, REQ, 128), BF),
        dma((NT,)), dma((NT,)), dma((NT,)), dma((NT,)),
        vmem((NY, ROWS, NZ * 256), BF),
        *[vmem((2, ROWS // 2, w), BF) for w in widths * 2],
        *[vmem((2, ROWS, w), BF) for w in widths * 2],
        *[vmem((ROWS, w), BF) for w in widths],
        vmem((ROWS, OUT), F32), dma((2, NQ)), dma((2, NQ)), dma((2, 2, NQ)), dma((2, 2, NQ)), dma((NQ,)),
    ]
    out = pl.pallas_call(
        kernel,
        out_shape=jax.ShapeDtypeStruct((ROWS, OUT), BF),
        in_specs=[hbm] * 12,
        out_specs=hbm,
        scratch_shapes=scratch,
        compiler_params=pltpu.CompilerParams(
            collective_id=0, has_side_effects=True, vmem_limit_bytes=60 * 2**20
        ),
        name="lora_projection",
    )(
        q.reshape(STEPS, REQ * HEADS, WIDTH),
        k.reshape(REQ * CACHE, WIDTH),
        v.reshape(REQ * CACHE, WIDTH),
        fk.reshape(STEPS, REQ, WIDTH),
        fv.reshape(STEPS, REQ, WIDTH),
        lens,
        wo,
        a.reshape(ADP * RANK, FEAT),
        b.reshape(ADP * 8, NT * OUT),
        table,
        fetch,
        entry,
    )
    return out.reshape(STEPS, REQ, OUT)


def solution(mesh):
    return jax.shard_map(
        on_device,
        mesh=mesh,
        in_specs=(
            P(None, "dp", "tensor", None),
            P("dp", "tensor", None, None),
            P("dp", "tensor", None, None),
            P(None, "dp", "tensor", None),
            P(None, "dp", "tensor", None),
            P("dp"),
            P("tensor", None),
            P("dp", None, "tensor"),
            P("dp", "tensor", None),
            P(),
            P("dp"),
            P("dp"),
        ),
        out_specs=P(None, "dp", "tensor"),
        check_vma=False,
    )
```

```python
import functools

import jax
import jax.numpy as jnp
from jax import lax
from jax.experimental import pallas as pl
from jax.experimental.pallas import tpu as pltpu
from jax.sharding import PartitionSpec as P

MESH = pl.DeviceIdType.MESH
BF = jnp.bfloat16
F32 = jnp.float32
I32 = jnp.int32

NZ, NY, NX, NT = 8, 4, 4, 8
STEPS, REQ, HEADS, WIDTH, CACHE = 4, 96, 8, 128, 48
ROWS = STEPS * REQ
FEAT = HEADS * WIDTH
RANK, ADP = 64, 4
OUT, SLOTS = 512, 32
PAIRS = REQ // 2
CHUNKS = ((0, 256, 2), (256, 256, 2))
NQ = len(CHUNKS)


def place():
    dp = lax.axis_index("dp")
    t = lax.axis_index("tensor")
    return dp // NY, dp % NY, t


def device(z, y, t):
    return {"dp": z * NY + y, "tensor": t}


def remote(src, dst, send, recv, to):
    return pltpu.make_async_remote_copy(
        src_ref=src, dst_ref=dst, send_sem=send, recv_sem=recv, device_id=to, device_id_type=MESH
    )


def kernel(
    q_hbm, k_hbm, v_hbm, fk_hbm, fv_hbm, len_hbm, wo_hbm, a_hbm, b_hbm, table_hbm, fetch_hbm, entry_hbm,
    o_hbm,
    len_ref, table_ref, fetch_ref, entry_ref, ssem, qv, kv, vv, fkv, fvv, fks, fvs, att, wo, lsem,
    ga, gb0, gb1, sa, ra, sb, rb, st, rt,
    xg, plr, sx, rx, sp, rp,
    cs, cr, own, xs, xd, sc, rc, sxd, rxd,
    acc, vsh, sh_src, sh_rcv, sh_all, s1, r1, s2, r2,
    ex, fs0, fs1, fr0, fr1, rs0, rs1, rr0, rr1, ov0, ov1, fin, farx, sf, rf, sr, rr, osem,
):
    gb = (gb0, gb1)
    far_src, far_rcv = (fs0, fs1), (fr0, fr1)
    ret_src, ret_rcv, ov = (rs0, rs1), (rr0, rr1), (ov0, ov1)
    z, y, t = place()
    x, c = t // 2, t % 2
    up, down = device((z + 1) % NZ, y, t), device((z + NZ - 1) % NZ, y, t)
    yup, ydown = device(z, (y + 1) % NY, t), device(z, (y + NY - 1) % NY, t)

    def y_peer(o):
        return device(z, (y + o) % NY, t)

    def t_peer(o):
        return device(z, y, (t + o) % NT)

    def x_peer(o):
        return device(z, y, ((x + o) % NX) * 2 + c)

    sibling = device(z, y, x * 2 + 1 - c)

    loads = [
        pltpu.make_async_copy(q_hbm, qv, lsem.at[0]),
        pltpu.make_async_copy(k_hbm, kv, lsem.at[1]),
        pltpu.make_async_copy(v_hbm, vv, lsem.at[2]),
        pltpu.make_async_copy(fk_hbm, fkv, lsem.at[3]),
        pltpu.make_async_copy(fv_hbm, fvv, lsem.at[4]),
        pltpu.make_async_copy(a_hbm, ga.at[z], lsem.at[5]),
        pltpu.make_async_copy(wo_hbm, wo, lsem.at[6]),
    ]
    own_b = [
        pltpu.make_async_copy(
            b_hbm.at[:, pl.ds(pl.multiple_of(t * OUT + first, 128), width)],
            gb[q].at[z, pl.ds(pl.multiple_of(t * 32, 32), 32)],
            lsem.at[7 + q],
        )
        for q, (first, width, _) in enumerate(CHUNKS)
    ]
    tables = [
        pltpu.make_async_copy(entry_hbm, entry_ref, ssem.at[0]),
        pltpu.make_async_copy(fetch_hbm, fetch_ref, ssem.at[1]),
        pltpu.make_async_copy(table_hbm, table_ref, ssem.at[2]),
        pltpu.make_async_copy(len_hbm, len_ref, ssem.at[3]),
    ]

    barrier = pltpu.get_barrier_semaphore()
    partners = [up, down] + [y_peer(o) for o in (1, 2, 3)] + [t_peer(o) for o in range(1, NT)]
    for to in partners:
        pl.semaphore_signal(barrier, inc=1, device_id=to, device_id_type=MESH)
    for copy in tables + loads + own_b:
        copy.start()
    pl.semaphore_wait(barrier, len(partners))

    def ring_block(d, k):
        return (z - k + NZ) % NZ if d == 0 else (z + k) % NZ

    def a_copy(d, k, h):
        b = ring_block(d, k)
        part = pl.ds(h * 128, 128)
        src = a_hbm.at[part] if k == 0 else ga.at[b, part]
        return remote(src, ga.at[b, part], sa.at[d, k, h], ra.at[d, k, h], up if d == 0 else down)

    def a_used(d, k, h):
        return k < 3 or h == d

    def a_send(k, i):
        for d, h in ((0, i), (1, 1 - i)):
            if a_used(d, k, h):
                if k > 0:
                    a_copy(d, k - 1, h).wait_recv()
                a_copy(d, k, h).start()

    def b_copy(d, k, q, h=None):
        if CHUNKS[q][2] == 2:
            rows = pl.ds((d if k == 3 else h) * 128, 128)
        else:
            rows = pl.ds(d * 128, 128) if k == 3 else pl.ds(0, 256)
        ref, part = gb[q].at[ring_block(d, k), rows], h or 0
        return remote(ref, ref, sb.at[d, k, q, part], rb.at[d, k, q, part], up if d == 0 else down)

    def b_send(k, q, i=None):
        for d in (0, 1):
            h = i if i is None or d == 0 else 1 - i
            if k > 0:
                b_copy(d, k - 1, q, d if k == 3 and CHUNKS[q][2] == 2 else h).wait_recv()
            b_copy(d, k, q, h).start()

    def b_arrived(q):
        for d in (0, 1):
            if CHUNKS[q][2] == 2:
                b_copy(d, 2, q, 1 - d).wait_recv()
            b_copy(d, 3, q).wait_recv()

    def b_sent(q):
        for d in (0, 1):
            for k in range(4):
                for h in (0, 1) if CHUNKS[q][2] == 2 and k < 3 else (None,):
                    b_copy(d, k, q, h).wait_send()

    def t_copy(o, q):
        first, width, _ = CHUNKS[q]
        return remote(
            b_hbm.at[:, pl.ds(pl.multiple_of(((t + o) % NT) * OUT + first, 128), width)],
            gb[q].at[z, pl.ds(pl.multiple_of(t * 32, 32), 32)],
            st.at[o, q], rt.at[o, q], t_peer(o),
        )

    def t_arrived(o, q):
        b = gb[q].at[z, pl.ds(pl.multiple_of(((t - o + NT) % NT) * 32, 32), 32)]
        remote(b, b, st.at[o, q], rt.at[o, q], t_peer(o)).wait_recv()

    a_send(0, 0)
    a_send(0, 1)
    for q in range(NQ):
        for o in range(1, NT):
            t_copy(o, q).start()

    def place_row(r, carry):
        plr[y, pl.ds(r, 1), :] = jnp.full((1, 128), table_ref[fetch_ref[entry_ref[r]]], I32)
        return carry

    for copy in tables:
        copy.wait()
    lax.fori_loop(0, REQ, place_row, 0, unroll=8)

    def p_copy(o):
        return remote(plr.at[y], plr.at[y], sp.at[o], rp.at[o], y_peer(o))

    def p_arrived(o):
        b = plr.at[(y - o + NY) % NY]
        remote(b, b, sp.at[o], rp.at[o], y_peer(o)).wait_recv()

    for o in (1, 2, 3):
        p_copy(o).start()

    for copy in loads[:5]:
        copy.wait()
    for u in range(STEPS):
        fks[pl.ds(u, REQ, stride=STEPS), :] = fkv[u].astype(F32)
        fvs[pl.ds(u, REQ, stride=STEPS), :] = fvv[u].astype(F32)

    row = lax.broadcasted_iota(I32, (64, 128), 0)
    col = lax.broadcasted_iota(I32, (64, 128), 1)
    row_step, row_req = row // 16, (row // 8) % 2
    cached, fresh = col < 96, (col >= 96) & (col < 104)
    same_cached = cached & ((col // CACHE) == row_req)
    same_fresh = fresh & (((col - 96) // STEPS) == row_req) & (((col - 96) % STEPS) <= row_step)
    position = jnp.where(same_cached, col % CACHE, jnp.where(same_fresh, 0, 1000))
    first = row_req == 0
    scale = WIDTH ** -0.5
    blank = jnp.zeros((24, 128), F32)

    def pair_group(ps):
        count = range(len(ps))
        eights = [pl.ds(pl.multiple_of(p * 8, 8), 8) for p in ps]
        rows = [pl.ds(pl.multiple_of(p * 96, 32), 96) for p in ps]
        sixteens = [pl.ds(pl.multiple_of(p * 16, 16), 16) for p in ps]

        def with_fresh(old, new, i):
            return jnp.concatenate(
                [old[rows[i], :], jnp.concatenate([new[eights[i], :], blank], 0).astype(BF)], 0
            )

        scores = [
            lax.dot_general(
                qv[:, sixteens[i], :].reshape(64, 128), with_fresh(kv, fks, i),
                (((1,), (1,)), ((), ())), preferred_element_type=F32,
            )
            for i in count
        ]
        live = [position < jnp.where(first, len_ref[2 * p], len_ref[2 * p + 1]) for p in ps]
        scores = [jnp.where(live[i], scores[i] * scale, -1e30) for i in count]
        highest = [jnp.max(v, axis=1, keepdims=True) for v in scores]
        powers = [jnp.exp(scores[i] - highest[i]) for i in count]
        sums = [jnp.sum(v, axis=1, keepdims=True) for v in powers]
        weights = [(powers[i] * (1.0 / sums[i])).astype(BF) for i in count]
        results = [
            jnp.dot(weights[i], with_fresh(vv, fvs, i), preferred_element_type=F32) for i in count
        ]
        for i in count:
            att[:, sixteens[i], :] = results[i].reshape(STEPS, 16, 128)

    def pairs(lo, hi, n):
        def some(i, carry):
            pair_group([lo + i * n + j for j in range(n)])
            return carry

        lax.fori_loop(0, (hi - lo) // n, some, 0)

    pairs(0, PAIRS // 2, 4)
    a_send(1, 0)
    pairs(PAIRS // 2, PAIRS, 4)
    for s in range(STEPS):
        for h in range(HEADS):
            xg[y, s * REQ:(s + 1) * REQ, h * WIDTH:(h + 1) * WIDTH] = att[
                s, pl.ds(h, REQ, stride=HEADS), :
            ].astype(BF)

    def x_copy(d, k):
        to = yup if d == 0 else ydown
        if k == 0:
            ref = xg.at[y]
        else:
            ref = xg.at[(y + 3) % NY if d == 0 else (y + 1) % NY, pl.ds(d * (ROWS // 2), ROWS // 2)]
        return remote(ref, ref, sx.at[d, k], rx.at[d, k], to)

    x_copy(0, 0).start()
    x_copy(1, 0).start()
    a_send(1, 1)

    loads[6].wait()

    def weight(i, core):
        return wo[:, pl.ds(pl.multiple_of((i * 2 + core) * OUT, OUT), OUT)]

    def for_sibling(i, carry):
        cs[i] = jnp.dot(xg[y], weight(i, 1 - c), preferred_element_type=F32).astype(BF)
        return carry

    def for_own(i, carry):
        own[i] = jnp.dot(xg[y], weight(i, c), preferred_element_type=F32)
        return carry

    lax.fori_loop(0, NX, for_sibling, 0)
    c_copy = remote(cs, cr, sc.at[0], rc.at[0], sibling)
    c_copy.start()
    lax.fori_loop(0, NX, for_own, 0)
    a_send(2, 0)
    c_copy.wait_recv()

    def xd_copy(o):
        return remote(xs.at[o], xd.at[o], sxd.at[o], rxd.at[o], x_peer(o))

    for o in (2, 1, 3):
        xs[o] = (own[(x + o) % NX] + cr[(x + o) % NX].astype(F32)).astype(BF)
        xd_copy(o).start()
    a_send(2, 1)

    lane = lax.broadcasted_iota(I32, (REQ, 128), 1)

    def index_of(b):
        p = plr[b]
        return jnp.where(((p >> 2) & 3) == y, ((p >> 4) << 2) | (p & 3), -1000)

    def shrink(yb, zb):
        full = lax.dot_general(xg[yb], ga[zb], (((1,), (1,)), ((), ())), preferred_element_type=F32)
        v = vsh[yb]
        lower, upper = v == 4 * zb, v == 4 * zb + 2
        for s in range(STEPS):
            part = full[s * REQ:(s + 1) * REQ]
            acc[yb, s * REQ:(s + 1) * REQ, :] += jnp.where(lower, part[:, :128], 0.0) + jnp.where(
                upper, part[:, 128:], 0.0
            )

    def shrinks(yb, blocks):
        for zb in blocks:
            shrink(yb, zb)

    acc[...] = jnp.zeros_like(acc)
    vsh[y] = index_of(y) - jnp.where(lane >= 64, 1, 0)
    for o in (1, 2, 3):
        p_arrived(o)
        b = (y - o + NY) % NY
        vsh[b] = index_of(b) - jnp.where(lane >= 64, 1, 0)
    loads[5].wait()

    near = [z, (z + 7) % NZ, (z + 1) % NZ]
    far = [(z + 6) % NZ, (z + 2) % NZ]
    last = [(z + 5) % NZ, (z + 3) % NZ]
    shrinks(y, near)
    for q in range(NQ):
        own_b[q].wait()
        for o in range(1, NT):
            t_arrived(o, q)
    b_send(0, 0, 0)
    x_copy(0, 0).wait_recv()
    x_copy(0, 1).start()
    x_copy(1, 0).wait_recv()
    x_copy(1, 1).start()
    a_send(3, 0)
    b_send(0, 0, 1)
    b_send(0, 1, 0)
    shrinks((y + 3) % NY, near)
    shrinks((y + 1) % NY, near)
    for yb in (y, (y + 3) % NY, (y + 1) % NY):
        shrinks(yb, far)
    x_copy(0, 1).wait_recv()
    x_copy(1, 1).wait_recv()
    shrinks((y + 2) % NY, near + far)
    b_send(1, 0, 0)
    b_send(1, 0, 1)
    a_copy(0, 2, 1).wait_recv()
    a_copy(1, 2, 0).wait_recv()
    for yb in range(NY):
        shrinks(yb, last)
    b_send(1, 1, 0)
    a_copy(0, 3, 0).wait_recv()
    a_copy(1, 3, 1).wait_recv()
    low = lax.broadcasted_iota(I32, (REQ, 128), 1) < 64

    def s1_copy(o):
        return remote(sh_src.at[(t + o) % NT], sh_rcv.at[o], s1.at[o], r1.at[o], t_peer(o))

    def give_share(j):
        o = (j - t + NT) % NT

        @pl.when(o != 0)
        def _():
            s1_copy(o).start()

    for b in range(2):
        shrinks(b, [(z + 4) % NZ])
        shrinks(b + 2, [(z + 4) % NZ])
        for s in range(STEPS):
            rows = pl.ds(s * REQ, REQ)
            a0, a1 = acc[b, rows, :], acc[b + 2, rows, :]
            a0 = a0 + pltpu.roll(a0, 64, 1)
            a1 = a1 + pltpu.roll(a1, 64, 1)
            sh_src[b * STEPS + s] = jnp.where(low, a0, a1).astype(BF)
        for s in range(STEPS):
            give_share(b * STEPS + s)
    b_send(2, 0, 0)
    b_send(2, 0, 1)
    b_send(0, 1, 1)
    fin[...] = own[x] + cr[x].astype(F32)
    for o in (1, 2, 3):
        xd_copy(o).wait_recv()
        fin[...] += xd[o].astype(F32)
    total = sh_src[t].astype(F32)
    for o in range(1, NT):
        s1_copy(o).wait_recv()
        total = total + sh_rcv[o].astype(F32)
    sh_all[t] = total.astype(BF)

    def s2_copy(o):
        return remote(sh_all.at[t], sh_all.at[t], s2.at[o], r2.at[o], t_peer(o))

    def s2_arrived(o):
        b = sh_all.at[(t - o + NT) % NT]
        remote(b, b, s2.at[o], r2.at[o], t_peer(o)).wait_recv()

    for o in (4, 3, 5, 2, 6, 1, 7):
        s2_copy(o).start()
    b_send(3, 0)
    b_send(2, 1, 0)
    b_send(1, 1, 1)
    for o in range(1, NT):
        s2_arrived(o)

    column = lax.broadcasted_iota(I32, (128, 256), 1)
    spread_row = lax.broadcasted_iota(I32, (128, 256), 0)
    adapter_of = (lax.broadcasted_iota(I32, (REQ, 256), 1) // 8) % ADP

    def spread(yb):
        half = yb // 2
        pick = jnp.where(
            spread_row == half * RANK + (column // 32) * 8 + column % 8, 1.0, 0.0
        ).astype(BF)
        index = index_of(yb)
        v = (jnp.concatenate([index, index], axis=1) - adapter_of).astype(F32).astype(BF)
        for s in range(STEPS):
            wide = jnp.dot(sh_all[(yb % 2) * STEPS + s], pick, preferred_element_type=F32).astype(BF)
            for zb in range(NZ):
                ex[yb, s * REQ:(s + 1) * REQ, zb * 256:(zb + 1) * 256] = jnp.where(
                    v == jnp.asarray(4 * zb, BF), wide, jnp.zeros_like(wide)
                )

    HALF = ROWS // 2
    top, bottom = pl.ds(0, HALF), pl.ds(HALF, HALF)

    def far_copy(d, q):
        return remote(far_src[q].at[d], far_rcv[q].at[d], sf.at[d, q], rf.at[d, q], yup if d == 0 else ydown)

    def ret_copy(d, h, q):
        rows = top if h == 0 else bottom
        return remote(
            ret_src[q].at[d, rows], ret_rcv[q].at[d, rows], sr.at[d, h, q], rr.at[d, h, q], yup if d == 0 else ydown
        )

    def columns(q):
        return slice(CHUNKS[q][0], CHUNKS[q][0] + CHUNKS[q][1])

    def expand(q, o):
        weights = gb[q][...].reshape(NZ * 256, CHUNKS[q][1])
        return jnp.dot(ex[(y + o) % NY], weights, preferred_element_type=F32)

    def expand_block(q, o, zb):
        cols = pl.ds(pl.multiple_of(zb * 256, 256), 256)
        return jnp.dot(ex[(y + o) % NY, :, cols], gb[q][zb], preferred_element_type=F32)

    def give_far(q, early=None):
        if early is None:
            value = expand(q, 2).astype(BF)
        else:
            value = (early[...] + expand_block(q, 2, (z + 4) % NZ)).astype(BF)
        for d in (0, 1):
            far_src[q][d] = value[d * HALF:(d + 1) * HALF]
            far_copy(d, q).start()

    def give_near(q):
        for d, o in ((0, 1), (1, 3)):
            ret_src[q][d] = expand(q, o).astype(BF)
            ret_copy(d, 1 - d, q).start()

    def pass_on(q):
        for d in (0, 1):
            far_copy(d, q).wait_recv()
            rows = top if d == 0 else bottom
            ret_src[q][d, rows, :] += far_rcv[q][d]
            ret_copy(d, d, q).start()

    def keep(q):
        fin[:, columns(q)] += expand(q, 0)

    spread((y + 2) % NY)
    b_arrived(0)
    give_far(0)
    spread((y + 1) % NY)
    spread((y + 3) % NY)
    b_send(3, 1)
    give_near(0)
    b_send(2, 1, 1)
    spread(y)
    keep(0)
    pass_on(0)
    for d in (0, 1):
        b_copy(d, 2, 1, 1 - d).wait_recv()
    farx[...] = expand_block(1, 2, z)
    for i in (1, 2, 3, 5, 6, 7):
        farx[...] += expand_block(1, 2, (z + i) % NZ)
    for d in (0, 1):
        b_copy(d, 3, 1).wait_recv()
    give_far(1, farx)
    give_near(1)
    keep(1)
    pass_on(1)
    writes = []
    for q in range(NQ):
        value = fin[:, columns(q)]
        for d in (0, 1):
            for h in (0, 1):
                ret_copy(d, h, q).wait_recv()
            value = value + ret_rcv[q][d].astype(F32)
        ov[q][...] = value.astype(BF)
        writes.append(pltpu.make_async_copy(ov[q], o_hbm.at[:, columns(q)], osem.at[q]))
        writes[q].start()

    for d in (0, 1):
        for k in range(4):
            for h in range(2):
                if a_used(d, k, h):
                    a_copy(d, k, h).wait_send()
        for k in range(2):
            x_copy(d, k).wait_send()
        for q in range(NQ):
            far_copy(d, q).wait_send()
            for h in (0, 1):
                ret_copy(d, h, q).wait_send()
    for q in range(NQ):
        b_sent(q)
    for o in range(1, NT):
        for q in range(NQ):
            t_copy(o, q).wait_send()
        s1_copy(o).wait_send()
        s2_copy(o).wait_send()
    for o in (1, 2, 3):
        p_copy(o).wait_send()
        xd_copy(o).wait_send()
    c_copy.wait_send()
    for copy in writes:
        copy.wait()


def on_device(q, k, v, fk, fv, lens, wo, a, b, table, fetch, entry):
    vmem, dma = pltpu.VMEM, pltpu.SemaphoreType.DMA
    hbm, smem = pl.BlockSpec(memory_space=pl.ANY), pltpu.SMEM
    widths = [w for _, w, _ in CHUNKS]
    scratch = [
        smem((REQ,), I32), smem((NY * NZ * ADP,), I32), smem((SLOTS,), I32), smem((REQ,), I32), dma((4,)),
        vmem((STEPS, REQ * HEADS, WIDTH), BF), vmem((REQ * CACHE, WIDTH), BF), vmem((REQ * CACHE, WIDTH), BF),
        vmem((STEPS, REQ, WIDTH), BF), vmem((STEPS, REQ, WIDTH), BF),
        vmem((ROWS, WIDTH), F32), vmem((ROWS, WIDTH), F32),
        vmem((STEPS, REQ * HEADS, WIDTH), F32), vmem((FEAT, NT * OUT), BF), dma((7 + NQ,)),
        vmem((NZ, 256, FEAT), BF), *[vmem((NZ, 256, w), BF) for w in widths],
        dma((2, 4, 2)), dma((2, 4, 2)), dma((2, 4, NQ, 2)), dma((2, 4, NQ, 2)), dma((NT, NQ)), dma((NT, NQ)),
        vmem((NY, ROWS, FEAT), BF), vmem((NY, REQ, 128), I32), dma((2, 2)), dma((2, 2)), dma((4,)), dma((4,)),
        vmem((NX, ROWS, OUT), BF), vmem((NX, ROWS, OUT), BF), vmem((NX, ROWS, OUT), F32),
        vmem((NX, ROWS, OUT), BF), vmem((NX, ROWS, OUT), BF), dma((1,)), dma((1,)), dma((4,)), dma((4,)),
        vmem((NY, ROWS, 128), F32), vmem((NY, REQ, 128), I32),
        vmem((NT, REQ, 128), BF), vmem((NT, REQ, 128), BF), vmem((NT, REQ, 128), BF),
        dma((NT,)), dma((NT,)), dma((NT,)), dma((NT,)),
        vmem((NY, ROWS, NZ * 256), BF),
        *[vmem((2, ROWS // 2, w), BF) for w in widths * 2],
        *[vmem((2, ROWS, w), BF) for w in widths * 2],
        *[vmem((ROWS, w), BF) for w in widths],
        vmem((ROWS, OUT), F32), vmem((ROWS, CHUNKS[1][1]), F32), dma((2, NQ)), dma((2, NQ)), dma((2, 2, NQ)), dma((2, 2, NQ)), dma((NQ,)),
    ]
    out = pl.pallas_call(
        kernel,
        out_shape=jax.ShapeDtypeStruct((ROWS, OUT), BF),
        in_specs=[hbm] * 12,
        out_specs=hbm,
        scratch_shapes=scratch,
        compiler_params=pltpu.CompilerParams(
            collective_id=0, has_side_effects=True, vmem_limit_bytes=60 * 2**20
        ),
        name="lora_projection",
    )(
        q.reshape(STEPS, REQ * HEADS, WIDTH),
        k.reshape(REQ * CACHE, WIDTH),
        v.reshape(REQ * CACHE, WIDTH),
        fk.reshape(STEPS, REQ, WIDTH),
        fv.reshape(STEPS, REQ, WIDTH),
        lens,
        wo,
        a.reshape(ADP * RANK, FEAT),
        b.reshape(ADP * 8, NT * OUT),
        table,
        fetch,
        entry,
    )
    return out.reshape(STEPS, REQ, OUT)


def solution(mesh):
    return jax.shard_map(
        on_device,
        mesh=mesh,
        in_specs=(
            P(None, "dp", "tensor", None),
            P("dp", "tensor", None, None),
            P("dp", "tensor", None, None),
            P(None, "dp", "tensor", None),
            P(None, "dp", "tensor", None),
            P("dp"),
            P("tensor", None),
            P("dp", None, "tensor"),
            P("dp", "tensor", None),
            P(),
            P("dp"),
            P("dp"),
        ),
        out_specs=P(None, "dp", "tensor"),
        check_vma=False,
    )
```
